1024 devices in a mesh: gx: 64 (over z_lo, y), gy: 16 (over x, z_hi, core).
Axes of the slice: x: 4, y: 8, z: 16 (z_hi: 2, z_lo: 8; z = z_hi * 8 + z_lo), core: 2. Of those that a mesh axis runs over, the one named last changes fastest.
Arguments:
- positions: float32 [3, 32768], P(None, ('gx', 'gy')), may hold values from -4 to 4
- species: int32 [32768], P(('gx', 'gy')), may hold values from 0 to 7
- atom_count: int32 [1024], P(('gx', 'gy')), may hold values from 10 to 32, as said below
- send_list: int32 [1024, 8, 4], P(('gx', 'gy')), may hold values from 0 to 31, as said below
- edges: int32 [1024, 2, 256], P(('gx', 'gy')), may hold values from 0 to 63, as said below
- centre_embed: float32 [512, 8], replicated, may hold values from -3 to 3
- neighbour_embed: float32 [512, 8], replicated, may hold values from -3 to 3
- radial_weight: float32 [512, 8], replicated, may hold values from -2 to 2
- env_weight: float32 [2, 64, 512], replicated, may hold values from -0.25 to 0.25
- latent_weight: float32 [2, 512, 704], replicated, may hold values from -0.21875 to 0.21875
- out_weight: float32 [512, 512], replicated, may hold values from -0.25 to 0.25
- head_weight: float32 [2, 512], replicated, may hold values from -0.25 to 0.25
Outputs:
- atom_energy: float32 [32768], P(('gx', 'gy'))
- forces: float32 [3, 32768], P(None, ('gx', 'gy'))
The draws below stay inside these ranges and needn't reach their ends.
Inputs may be any that keep to these rules, and one draw needn't show every extreme that they name: Device p's live atoms are its slots 0 to atom_count[p] - 1, the rest are padding; its live edges are its first 8 atom_count[p] edge slots. send_list[p, k, g] is a live atom of device p; the 4 atoms of one (p, k) are distinct and are sent to the device at offset k. `edges`: row 0 is a live atom slot of the device; row 1 is a live atom slot other than the centre, or a ghost slot 32 + k * 4 + g.
All inputs are finite; a program needn't handle non-finite values.
Results may differ from the reference program's by a relative error of at most 0.00025.
Values sent between devices are 32-bit elements; how exact they have to be, the bound alone decides.
A program may use at most 32 MiB of HBM per device.

```python
import math
import jax
import jax.numpy as jnp
from jax import lax

TENSOR = 64
LATENT = 512
HARM = 9
BASIS = 8
SPECIES = 8
LAYERS = 2
ATOM_DEV = 32
GHOST = 4
EDGES = 256
ATOMS = 32768
N_GX = 64
N_GY = 16


def count_draw(key):
    key = jax.random.fold_in(key, 101)
    devices = ATOMS // ATOM_DEV
    lowest = ATOM_DEV // 3
    key_level, key_full, key_low = jax.random.split(key, 3)
    level = jax.random.randint(key_level, (devices,), 0, 33)
    counts = lowest + (ATOM_DEV - lowest) * level * level * level // 32768
    full_at = jax.random.randint(key_full, (), 0, devices)
    low_at = (full_at + 1 + jax.random.randint(key_low, (), 0, devices - 1)) % devices
    counts = counts.at[full_at].set(ATOM_DEV)
    counts = counts.at[low_at].set(lowest)
    return counts.astype(jnp.int32)


def draw_atom_count(key, part):
    counts = count_draw(key)
    return counts


def draw_send_list(key, part):
    counts = count_draw(key)
    key = jax.random.fold_in(key, 7)
    devices = ATOMS // ATOM_DEV
    place = jnp.arange(ATOM_DEV, dtype=jnp.int32)[None, None, :]
    scores = jax.random.randint(key, (devices, 8, ATOM_DEV), 0, 2 ** 19) * ATOM_DEV + place
    limit = counts[:, None, None]
    scores = jnp.where(place == limit - 1, 2 ** 30, scores)
    scores = jnp.where(place == 0, 2 ** 30 - 1, scores)
    scores = jnp.where(place >= limit, -1, scores)
    _, chosen = lax.top_k(scores, GHOST)
    return chosen.astype(jnp.int32)


def draw_edges(key, part):
    counts = count_draw(key)
    key = jax.random.fold_in(key, 13)
    devices = ATOMS // ATOM_DEV
    key_centre, key_step, key_ghost, key_pick = jax.random.split(key, 4)
    limit = counts[:, None]
    centre = jax.random.randint(key_centre, (devices, EDGES), 0, limit)
    centre = centre.at[:, 0].set(0)
    step = jax.random.randint(key_step, (devices, EDGES), 0, limit - 1)
    partner = (centre + 1 + step) % limit
    ghost = jax.random.randint(key_ghost, (devices, EDGES), 0, 8 * GHOST)
    pick = jax.random.randint(key_pick, (devices, EDGES), 0, 2)
    other = jnp.where(pick == 1, ATOM_DEV + ghost, partner)
    other = other.at[:, EDGES - 1].set(ATOM_DEV + 8 * GHOST - 1)
    return jnp.stack([centre, other], axis=1).astype(jnp.int32)


def with_ends(result, rng, smallest, largest):
    spot = [jax.random.randint(jax.random.fold_in(rng, axis), (), 0, length) for axis, length in enumerate(result.shape)]
    longest = result.shape.index(max(result.shape))
    beside = spot[:longest] + [(spot[longest] + 1) % result.shape[longest]] + spot[longest + 1:]
    return result.at[tuple(spot)].set(smallest).at[tuple(beside)].set(largest)


def level_of(own_key, extent, pieces, low, high):
    factor_of = 1.0
    for dim, shards_of in pieces:
        draws = jax.random.uniform(jax.random.fold_in(jax.random.fold_in(own_key, 6), dim), (shards_of,), jnp.float32, low / len(pieces), high / len(pieces))
        factor_of = factor_of * jnp.repeat(jnp.exp(draws), extent[dim] // shards_of).reshape((-1,) + (1,) * (len(extent) - 1 - dim))
    return factor_of


def normal_values(rng, shape, scale, most, cuts=(), held_as=jnp.bfloat16):
    factor_of = level_of(rng, shape, cuts, -0.22, 0.18) if cuts else 1.0
    values = jax.random.normal(rng, shape, jnp.float32) * scale * factor_of
    return jnp.minimum(jnp.maximum(values, -most), most).astype(held_as)


def setup_inputs(seed: int = 0) -> dict:
    key_of = jax.random.split(jax.random.key(seed), 13)
    return {
        "positions": normal_values(key_of[0], (3, ATOMS), 0.7, 4.0, ((1, 1024),), jnp.float32),
        "species": with_ends(jax.random.randint(key_of[1], (ATOMS,), 0, SPECIES), jax.random.fold_in(key_of[1], 1), 0, SPECIES - 1).astype(jnp.int32),
        "atom_count": draw_atom_count(jax.random.fold_in(key_of[12], 71), 0),
        "send_list": draw_send_list(jax.random.fold_in(key_of[12], 71), 0),
        "edges": draw_edges(jax.random.fold_in(key_of[12], 71), 0),
        "centre_embed": normal_values(key_of[5], (LATENT, SPECIES), 0.5, 3.0, (), jnp.float32),
        "neighbour_embed": normal_values(key_of[6], (LATENT, SPECIES), 0.5, 3.0, (), jnp.float32),
        "radial_weight": normal_values(key_of[7], (LATENT, BASIS), BASIS ** -0.5, 2.0, (), jnp.float32),
        "env_weight": normal_values(key_of[8], (LAYERS, TENSOR, LATENT), LATENT ** -0.5, 0.25, (), jnp.float32),
        "latent_weight": normal_values(key_of[9], (LAYERS, LATENT, LATENT + 3 * TENSOR), (LATENT + 3 * TENSOR) ** -0.5, 0.21875, (), jnp.float32),
        "out_weight": normal_values(key_of[10], (LATENT, LATENT), LATENT ** -0.5, 0.25, (), jnp.float32),
        "head_weight": normal_values(key_of[11], (2, LATENT), LATENT ** -0.5, 0.25, (), jnp.float32),
    }


offset_x = (-1, -1, -1, 0, 0, 1, 1, 1)
offset_y = (-1, 0, 1, -1, 1, -1, 0, 1)
highest = lax.Precision.HIGHEST

def parity():
    return jnp.array([1.0, -1.0, -1.0, -1.0, 1.0, 1.0, 1.0, 1.0, 1.0], dtype=jnp.float32)

def harmonics(unit):
    root = math.sqrt(3.0)
    along_x, along_y, along_z = (unit[0], unit[1], unit[2])
    return jnp.stack([jnp.ones_like(along_x), along_x, along_y, along_z, root * along_x * along_y, root * along_y * along_z, 0.5 * (3.0 * along_z * along_z - 1.0), root * along_x * along_z, 0.5 * root * (along_x * along_x - along_y * along_y)])

def geometry(start, finish, count_basis):
    offset = finish - start
    squared = lax.optimization_barrier(jnp.sum(offset * offset, axis=0))
    unit = offset / jnp.sqrt(1.0 + squared)
    length = jnp.sqrt(squared)
    centres = 0.5 * jnp.arange(count_basis, dtype=jnp.float32)
    basis = jnp.exp(-2.0 * (length[None, :] - centres[:, None]) ** 2)
    return (unit, basis, harmonics(unit))

def refine(hidden, env_centre, env_other, harm, weight):
    sign = parity()[None, :, None]
    product = (env_centre + env_other * sign) * harm[None]
    scalars = jnp.concatenate([hidden, product[:, 0], lax.optimization_barrier(jnp.sum(product[:, 1:4], axis=1)), lax.optimization_barrier(jnp.sum(product[:, 4:9], axis=1))], axis=0)
    return hidden + jax.nn.silu(jnp.dot(weight, scalars, precision=highest))

def reference(positions, species, atom_count, send_list, edges, centre_embed, neighbour_embed, radial_weight, env_weight, latent_weight, out_weight, head_weight):
    devices = N_GX * N_GY
    place = jnp.arange(devices, dtype=jnp.int32)
    row_x = place // N_GY
    row_y = place % N_GY
    step_x = jnp.array(offset_x, dtype=jnp.int32)
    step_y = jnp.array(offset_y, dtype=jnp.int32)
    source = (row_x[:, None] + step_x[None, :]) % N_GX * N_GY + (row_y[:, None] + step_y[None, :]) % N_GY
    back = 7 - jnp.arange(8, dtype=jnp.int32)
    ghost_atom = source[:, :, None] * ATOM_DEV + send_list[source, back[None, :]]
    own_slots = place[:, None] * ATOM_DEV + jnp.arange(ATOM_DEV, dtype=jnp.int32)[None, :]
    slots = jnp.concatenate([own_slots, ghost_atom.reshape(devices, 8 * GHOST)], axis=1).astype(jnp.int32)
    centre = (place[:, None] * ATOM_DEV + edges[:, 0, :]).astype(jnp.int32)
    other = jnp.take_along_axis(slots, edges[:, 1, :].astype(jnp.int32), axis=1).astype(jnp.int32)
    per_atom = EDGES // ATOM_DEV
    live = (jnp.arange(EDGES, dtype=jnp.int32)[None, :] < per_atom * atom_count[:, None]).astype(jnp.float32)
    parity_rows = jnp.tile(parity(), TENSOR)[:, None]

    def initial(pair):
        centre_ids, other_ids = pair
        unit, basis, harm = geometry(positions[:, centre_ids], positions[:, other_ids], BASIS)
        inner = jnp.dot(radial_weight, basis, precision=highest)
        inner = inner + centre_embed[:, species[centre_ids]] + neighbour_embed[:, species[other_ids]]
        return jax.nn.silu(inner)
    hidden = lax.map(initial, (centre, other))
    for layer in range(LAYERS):

        def accumulate(env, inputs):
            block, centre_ids, other_ids, alive = inputs
            unit, basis, harm = geometry(positions[:, centre_ids], positions[:, other_ids], BASIS)
            weights_e = jnp.dot(env_weight[layer], block, precision=highest)
            contrib = (weights_e[:, None, :] * harm[None]).reshape(TENSOR * HARM, EDGES) * (alive * 0.25)
            env = env.at[:, centre_ids].add(contrib)
            env = env.at[:, other_ids].add(contrib * parity_rows)
            return (env, None)
        env, _ = lax.scan(accumulate, jnp.zeros((TENSOR * HARM, ATOMS), jnp.float32), (hidden, centre, other, live))

        def update(inputs):
            block, centre_ids, other_ids = inputs
            unit, basis, harm = geometry(positions[:, centre_ids], positions[:, other_ids], BASIS)
            env_centre = env[:, centre_ids].reshape(TENSOR, HARM, EDGES)
            env_other = env[:, other_ids].reshape(TENSOR, HARM, EDGES)
            return refine(block, env_centre, env_other, harm, latent_weight[layer])
        hidden = lax.map(update, (hidden, centre, other))

    def finish_sums(totals, inputs):
        block, centre_ids, other_ids, alive = inputs
        unit, basis, harm = geometry(positions[:, centre_ids], positions[:, other_ids], BASIS)
        latent = jax.nn.silu(jnp.dot(out_weight, block, precision=highest))
        heads = jnp.dot(head_weight, latent, precision=highest)
        energy_e = 0.5 * heads[0] * alive
        push = heads[1] * alive * unit
        totals = totals.at[:, centre_ids].add(jnp.concatenate([energy_e[None], push], axis=0))
        totals = totals.at[:, other_ids].add(jnp.concatenate([energy_e[None], -push], axis=0))
        return (totals, None)
    totals, _ = lax.scan(finish_sums, jnp.zeros((4, ATOMS), jnp.float32), (hidden, centre, other, live))
    return (totals[0], totals[1:4])
```

```python
import functools

import jax
import jax.numpy as jnp
from jax import lax
from jax.experimental import pallas as pl
from jax.experimental.pallas import tpu as pltpu
from jax.sharding import PartitionSpec as P

MESH = pl.DeviceIdType.MESH
F32 = jnp.float32
BF16 = jnp.bfloat16
OFFSETS = ((-1, -1), (-1, 0), (-1, 1), (0, -1), (0, 1), (1, -1), (1, 0), (1, 1))
AROUND = OFFSETS + ((0, 0),)
ROOT3 = 3.0 ** 0.5


def host(lx, ly):
    a, b = (72 - lx) % 64, (28 - ly) % 16
    x, zz = a // 16, a % 16
    z = zz + (x % 2) * (15 - 2 * zz)
    y, core = b // 2, b % 2
    return (z % 8) * 8 + y, x * 4 + (z // 8) * 2 + core


def column(gx, gy):
    y, x, core = gx % 8, gy // 4, gy % 2
    z = ((gy // 2) % 2) * 8 + gx // 8
    zz = z + (x % 2) * (15 - 2 * z)
    return (72 - (x * 16 + zz)) % 64, (28 - (y * 2 + core)) % 16


def iota(shape, dim):
    return lax.broadcasted_iota(jnp.int32, shape, dim)


def mm(a, b):
    return lax.dot_general(a, b, (((1,), (0,)), ((), ())), preferred_element_type=F32)


def mm_nt(a, b):
    return lax.dot_general(a, b, (((1,), (1,)), ((), ())), preferred_element_type=F32)


def top(x):
    return x.astype(BF16).astype(F32)


def split(x):
    hi = x.astype(BF16)
    return hi, (x - hi.astype(F32)).astype(BF16)


def stack3(x):
    a = top(x)
    b = top(x - a)
    return jnp.concatenate([a, b, x - a - b], axis=0).astype(BF16)


def unstack3(y, n):
    return y[:n] + y[n : 2 * n] + y[2 * n : 3 * n]


def silu(v):
    return v / (1.0 + jnp.exp(-v))


def kernel(
    nx, ny, pos_ref, spc_ref, cnt_ref, snd_ref, edg_ref, emb_c, emb_n, rad_w, env_w, lat_w, out_w, head_ref,
    energy_ref, force_ref,
    embc_v, embn_v, rad_v, env_v, lat_v, out_v,
    feat_w, expand_w, env_cat, lat_cat, sca_cat, out_cat,
    tile_near, tile_own, got_near, got_own, got_edges,
    send_part, got_part, send_env, got_env, tile_tot, got_tot,
    hid_cat, hid, pre, harm_x,
    w_sem, near_s, near_r, own_s, own_r, part_s, part_r, env_s, env_r, tot_s, tot_r,
):
    gx, gy = lax.axis_index("gx"), lax.axis_index("gy")
    lx, ly = column(gx, gy)
    beside = [((lx + dx + nx) % nx, (ly + dy + ny) % ny) for dx, dy in AROUND]
    hosts = [host(*b) for b in beside]
    targets = [host((gx + dx + nx) % nx, (gy + dy + ny) % ny) for dx, dy in AROUND]

    barrier = pltpu.get_barrier_semaphore()
    for k in range(8):
        pl.semaphore_signal(barrier, inc=1, device_id=hosts[k], device_id_type=MESH)
    for k in range(9):
        pl.semaphore_signal(barrier, inc=1, device_id=beside[k], device_id_type=MESH)

    loads = [
        pltpu.make_async_copy(src, dst, w_sem.at[i])
        for i, (src, dst) in enumerate(
            ((emb_c, embc_v), (emb_n, embn_v), (rad_w, rad_v), (env_w, env_v), (lat_w, lat_v), (out_w, out_v))
        )
    ]
    for load in loads:
        load.start()

    lane = iota((1, 128), 1)
    spread_k = ((iota((8, 128), 1) - 32) // 4 == iota((8, 128), 0)) & (iota((8, 128), 1) >= 32)
    by_lane = mm(snd_ref[0].astype(F32).astype(BF16), spread_k.astype(F32).astype(BF16))
    by_lane = jnp.where(iota((4, 128), 1) % 4 == iota((4, 128), 0), by_lane, 0.0)
    names = jnp.sum(by_lane, axis=0, keepdims=True)
    names = jnp.where(lane < 32, lane.astype(F32), jnp.where(lane < 64, names, -1.0))
    pick = (iota((32, 128), 0).astype(F32) == names).astype(F32)
    atoms = jnp.concatenate([pos_ref[...], spc_ref[...].astype(F32), jnp.zeros((4, 32), F32)], axis=0)
    picked = unstack3(mm(stack3(atoms), pick.astype(BF16)), 8)
    tile_near[...] = picked[:4]
    count_row = jnp.broadcast_to(cnt_ref[...].astype(F32), (1, 128))
    tile_own[...] = jnp.concatenate([picked[:4], names, count_row, names, names], axis=0)

    pl.semaphore_wait(barrier, 17)

    def remote(src, dst, send_sem, recv_sem, device):
        return pltpu.make_async_remote_copy(
            src_ref=src, dst_ref=dst, send_sem=send_sem, recv_sem=recv_sem, device_id=device, device_id_type=MESH
        )

    first = [
        remote(edg_ref, got_edges, own_s.at[0], own_r.at[0], targets[8]),
        remote(tile_own, got_own, own_s.at[1], own_r.at[1], targets[8]),
    ]
    first += [remote(tile_near, got_near.at[k], near_s.at[k], near_r.at[k], targets[k]) for k in range(8)]
    for copy in first:
        copy.start()

    for load in loads[:3]:
        load.wait()
    r, c, n = rad_v[...], embc_v[...], embn_v[...]
    feat_w[...] = jnp.concatenate(
        [top(r), r - top(r), top(r), top(c), c - top(c), top(n), n - top(n), jnp.zeros((72, 512), F32)], axis=0
    ).astype(BF16)
    row, col = iota((128, 640), 0), iota((128, 640), 1)
    expand_w[...] = ((row >= 64) & (row < 112) & (row % 16 == col // 64)).astype(F32).astype(BF16)
    loads[3].wait()
    for layer in range(2):
        e = 0.25 * env_v[layer]
        hi, lo = split(jnp.concatenate([e, e], axis=0).T)
        env_cat[layer, 0:512] = hi
        env_cat[layer, 512:1024] = hi
        env_cat[layer, 1024:1536] = lo
    loads[4].wait()

    def cut_latent(i, carry):
        layer, at = i // 8, pl.multiple_of((i % 8) * 64, 64)
        hi, lo = split(lat_v[layer, pl.ds(at, 64), :])
        lat_cat[layer, pl.ds(at, 64), :] = hi
        lat_cat[layer, pl.ds(pl.multiple_of(512 + at, 64), 64), :] = hi
        lat_cat[layer, pl.ds(pl.multiple_of(1024 + at, 64), 64), :] = lo
        return carry

    lax.fori_loop(0, 16, cut_latent, 0)
    for layer in range(2):
        for i, at in enumerate((576, 640, 512, 640)):
            hi, lo = split(lat_v[layer, at : at + 64, :])
            sca_cat[layer, 64 * i : 64 * i + 64] = hi
            sca_cat[layer, 256 + 64 * i : 320 + 64 * i] = hi
            sca_cat[layer, 512 + 64 * i : 576 + 64 * i] = lo
    loads[5].wait()
    for i in range(4):
        hi, lo = split(out_v[128 * i : 128 * i + 128, :].T)
        out_cat[0:512, 128 * i : 128 * i + 128] = hi
        out_cat[512:1024, 128 * i : 128 * i + 128] = hi
        out_cat[1024:1536, 128 * i : 128 * i + 128] = lo

    for copy in first:
        copy.wait_recv()

    own = got_own[...]
    pool = jnp.where(lane < 32, own[:4], 0.0)
    for k in range(8):
        pool = jnp.where((lane >= 32 + 4 * k) & (lane < 36 + 4 * k), got_near[k], pool)
    names = own[4:5]
    live = iota((1, 256), 1).astype(F32) < 8.0 * jnp.concatenate([own[5:6], own[5:6]], axis=1)
    ends = got_edges[0]
    ends = jnp.where(ends < 32, ends, 92 - ends + 2 * (ends & 3))
    ends = jnp.where(live, ends, -1)
    slot = iota((64, 256), 0)
    is_c = (slot == ends[0:1]).astype(F32)
    is_o = (slot == ends[1:2]).astype(F32)
    plus, minus = is_c + is_o, is_c - is_o
    coords = stack3(jnp.concatenate([pool, jnp.zeros((4, 128), F32)], axis=0)[:, :64])
    at_c = unstack3(mm(coords, is_c.astype(BF16)), 8)
    at_o = unstack3(mm(coords, is_o.astype(BF16)), 8)
    diff = at_o - at_c
    dx, dy, dz = diff[0:1], diff[1:2], diff[2:3]
    squared = dx * dx + dy * dy + dz * dz
    scale = 1.0 / jnp.sqrt(1.0 + squared)
    ux, uy, uz = dx * scale, dy * scale, dz * scale
    length = jnp.sqrt(squared)
    step = length - 0.5 * iota((8, 256), 0).astype(F32)
    basis = jnp.exp(-2.0 * step * step)
    kinds = iota((8, 256), 0).astype(F32)
    hot_c = (at_c[3:4] == kinds).astype(F32)
    hot_o = (at_o[3:4] == kinds).astype(F32)
    harm = jnp.concatenate(
        [
            jnp.ones_like(ux), ROOT3 * ux * uy, ROOT3 * uy * uz, 0.5 * (3.0 * uz * uz - 1.0), ROOT3 * ux * uz,
            0.5 * ROOT3 * (ux * ux - uy * uy), ux, uy, uz, jnp.zeros((7, 256), F32),
        ],
        axis=0,
    )
    h1 = top(harm)
    h2 = top(harm - h1)
    b1 = top(basis)
    feat = jnp.concatenate(
        [
            b1, b1, basis - b1, hot_c, hot_c, hot_o, hot_o, jnp.zeros((8, 256), F32),
            h1, h2, harm - h1 - h2, jnp.zeros((16, 256), F32),
        ],
        axis=0,
    ).T.astype(BF16)
    hid[...] = silu(mm(feat, feat_w[...]))
    harm_x[...] = mm(feat, expand_w[...])

    put_p = jnp.concatenate([plus, plus], axis=1).astype(BF16)
    put_m = jnp.concatenate([minus, minus], axis=1).astype(BF16)
    get_p = jnp.concatenate([plus, plus], axis=0).T.astype(BF16)
    get_m = jnp.concatenate([minus, minus], axis=0).T.astype(BF16)

    def keep_hidden():
        hi, lo = split(hid[...])
        hid_cat[:, 0:512] = hi
        hid_cat[:, 512:1024] = lo
        hid_cat[:, 1024:1536] = hi

    keep_hidden()
    same = None
    copies = []
    for layer in range(2):
        w = mm(hid_cat[...], env_cat[layer])
        contrib = jnp.concatenate([w] * 5, axis=1) * harm_x[...]
        hi, lo = split(contrib)
        both = jnp.concatenate([hi, lo], axis=0)
        part_p, part_m = mm(put_p, both[:, :384]), mm(put_m, both[:, 384:])
        part = jnp.concatenate([part_p, part_m], axis=1)
        for k in range(8):
            send_part[layer, k] = part[32 + 4 * k : 36 + 4 * k]
        back = [
            remote(
                send_part.at[layer, k], got_part.at[layer, k], part_s.at[layer, k], part_r.at[layer, k], hosts[7 - k]
            )
            for k in range(8)
        ]
        for copy in back:
            copy.start()
        copies += back
        if same is None:
            names_col = own.T[:, 4:5]
            same = (names_col[:64] == names).astype(F32)[:, :64]
            same = jnp.concatenate([same, same], axis=1).astype(BF16)
        pre[...] = mm(hid_cat[...], lat_cat[layer])
        for copy in back:
            copy.wait_recv()
        got = got_part[layer].reshape(32, 640)
        hi, lo = split(jnp.concatenate([part[:32], got], axis=0))
        env = mm(same, jnp.concatenate([hi, lo], axis=0))
        for k in range(8):
            send_env[layer, k] = env[32 + 4 * k : 36 + 4 * k]
        forth = [
            remote(send_env.at[layer, k], got_env.at[layer, k], env_s.at[layer, k], env_r.at[layer, k], hosts[k])
            for k in range(8)
        ]
        for copy in forth:
            copy.start()
        copies += forth
        for copy in forth:
            copy.wait_recv()
        got = got_env[layer].reshape(32, 640)
        hi, lo = split(jnp.concatenate([env[:32], got], axis=0))
        both = jnp.concatenate([hi, lo], axis=0)
        prod = jnp.concatenate([mm(get_p, both[:, :384]), mm(get_m, both[:, 384:])], axis=1) * harm_x[...]
        t0, t1, t2, t3, t4 = [prod[:, 128 * i : 128 * i + 128] for i in range(5)]
        t12 = t1 + t2
        low = iota((256, 128), 1) < 64
        fold = jnp.where(low, t3 + pltpu.roll(t3, 64, 1) + t4, t12 + pltpu.roll(t12, 64, 1))
        hi, lo = split(jnp.concatenate([fold, t0], axis=1))
        hid[...] += silu(pre[...] + mm(jnp.concatenate([hi, lo, hi], axis=1), sca_cat[layer]))
        keep_hidden()

    hi, lo = split(silu(mm(hid_cat[...], out_cat[...])))
    h = head_ref[...]
    hh = top(h)
    hw = jnp.concatenate([hh, h - hh, jnp.zeros((4, 512), F32)], axis=0).astype(BF16)
    by_hi, by_lo = mm_nt(hw, hi), mm_nt(hw, lo)
    heads = by_hi[0:2] + by_hi[2:4] + by_lo[0:2]
    push = heads[1:2]
    vals = jnp.concatenate([0.5 * heads[0:1], push * ux, push * uy, push * uz, jnp.zeros((4, 256), F32)], axis=0)
    vals = stack3(vals)
    tot_p, tot_m = unstack3(mm(vals, get_p), 8), unstack3(mm(vals, get_m), 8)
    tile_tot[...] = jnp.where(iota((4, 128), 0) == 0, tot_p[:4], tot_m[:4])
    last = [remote(tile_tot, got_tot.at[k], tot_s.at[k], tot_r.at[k], beside[7 - k]) for k in range(8)]
    last.append(remote(tile_tot, got_tot.at[8], tot_s.at[8], tot_r.at[8], beside[8]))
    for copy in last:
        copy.start()
    for copy in first + copies:
        copy.wait_send()
    for copy in last:
        copy.wait_recv()
    total = jnp.where(lane < 32, got_tot[8], 0.0)
    for k in range(8):
        total = jnp.where((lane >= 32 + 4 * k) & (lane < 36 + 4 * k), got_tot[k], total)
    total = stack3(jnp.concatenate([total, jnp.zeros((4, 128), F32)], axis=0))
    out = unstack3(mm_nt(total, pick.astype(BF16)), 8)
    energy_ref[...] = out[0:1]
    force_ref[...] = out[1:4]
    for copy in last:
        copy.wait_send()


def solution(mesh):
    nx, ny = mesh.shape["gx"], mesh.shape["gy"]

    def local(
        positions, species, atom_count, send_list, edges, centre_embed, neighbour_embed, radial_weight, env_weight,
        latent_weight, out_weight, head_weight,
    ):
        vmem, anywhere = pl.BlockSpec(memory_space=pltpu.VMEM), pl.BlockSpec(memory_space=pl.ANY)
        dma = pltpu.SemaphoreType.DMA
        energy, forces = pl.pallas_call(
            functools.partial(kernel, nx, ny),
            out_shape=(jax.ShapeDtypeStruct((1, 32), F32), jax.ShapeDtypeStruct((3, 32), F32)),
            in_specs=[vmem] * 5 + [anywhere] * 6 + [vmem],
            out_specs=(vmem, vmem),
            scratch_shapes=[
                pltpu.VMEM((8, 512), F32), pltpu.VMEM((8, 512), F32), pltpu.VMEM((8, 512), F32),
                pltpu.VMEM((2, 64, 512), F32), pltpu.VMEM((2, 704, 512), F32), pltpu.VMEM((512, 512), F32),
                pltpu.VMEM((128, 512), BF16), pltpu.VMEM((128, 640), BF16), pltpu.VMEM((2, 1536, 128), BF16),
                pltpu.VMEM((2, 1536, 512), BF16), pltpu.VMEM((2, 768, 512), BF16), pltpu.VMEM((1536, 512), BF16),
                pltpu.VMEM((4, 128), F32), pltpu.VMEM((8, 128), F32), pltpu.VMEM((8, 4, 128), F32),
                pltpu.VMEM((8, 128), F32), pltpu.VMEM((1, 2, 256), jnp.int32),
                pltpu.VMEM((2, 8, 4, 640), F32), pltpu.VMEM((2, 8, 4, 640), F32),
                pltpu.VMEM((2, 8, 4, 640), F32), pltpu.VMEM((2, 8, 4, 640), F32),
                pltpu.VMEM((4, 128), F32), pltpu.VMEM((9, 4, 128), F32),
                pltpu.VMEM((256, 1536), BF16), pltpu.VMEM((256, 512), F32), pltpu.VMEM((256, 512), F32),
                pltpu.VMEM((256, 640), F32),
                dma((6,)), dma((8,)), dma((8,)), dma((2,)), dma((2,)), dma((2, 8)), dma((2, 8)), dma((2, 8)),
                dma((2, 8)), dma((9,)), dma((9,)),
            ],
            compiler_params=pltpu.CompilerParams(
                collective_id=0, has_side_effects=True, vmem_limit_bytes=48 * 1024 * 1024
            ),
            name="pair_network",
        )(
            positions, species.reshape(1, -1), atom_count.reshape(1, 1), send_list.transpose(0, 2, 1), edges,
            centre_embed.T, neighbour_embed.T, radial_weight.T, env_weight, latent_weight.transpose(0, 2, 1),
            out_weight, head_weight,
        )
        return energy.reshape(-1), forces

    placed = (
        P(None, ("gx", "gy")), P(("gx", "gy")), P(("gx", "gy")), P(("gx", "gy"), None, None),
        P(("gx", "gy"), None, None), P(), P(), P(), P(), P(), P(), P(),
    )
    return jax.shard_map(
        local, mesh=mesh, in_specs=placed, out_specs=(P(("gx", "gy")), P(None, ("gx", "gy"))), check_vma=False
    )
```

```python
import functools

import jax
import jax.numpy as jnp
from jax import lax
from jax.experimental import pallas as pl
from jax.experimental.pallas import tpu as pltpu
from jax.sharding import PartitionSpec as P

MESH = pl.DeviceIdType.MESH
F32 = jnp.float32
BF16 = jnp.bfloat16
OFFSETS = ((-1, -1), (-1, 0), (-1, 1), (0, -1), (0, 1), (1, -1), (1, 0), (1, 1))
AROUND = OFFSETS + ((0, 0),)
ORDER = (0, 2, 5, 7, 1, 6, 3, 4)
ROOT3 = 3.0 ** 0.5


def host(lx, ly):
    a, b = (lx + 8) % 64, (ly + 2) % 16
    zi, yy, t = a // 8, a % 8, b // 2
    x = t // 2
    z = 2 * zi + (t + x) % 2
    y = yy + (zi % 2) * (7 - 2 * yy)
    return (z % 8) * 8 + y, x * 4 + (z // 8) * 2 + b % 2


def column(gx, gy):
    y, x = gx % 8, gy // 4
    z = ((gy // 2) % 2) * 8 + gx // 8
    zi = z // 2
    a = 8 * zi + y + (zi % 2) * (7 - 2 * y)
    b = 4 * x + 2 * ((z + x) % 2) + gy % 2
    return (a + 56) % 64, (b + 14) % 16


def iota(shape, dim):
    return lax.broadcasted_iota(jnp.int32, shape, dim)


def mm(a, b):
    return lax.dot_general(a, b, (((1,), (0,)), ((), ())), preferred_element_type=F32)


def mm_nt(a, b):
    return lax.dot_general(a, b, (((1,), (1,)), ((), ())), preferred_element_type=F32)


def top(x):
    return x.astype(BF16).astype(F32)


def split(x):
    hi = x.astype(BF16)
    return hi, (x - hi.astype(F32)).astype(BF16)


def stack3(x):
    a = top(x)
    b = top(x - a)
    return jnp.concatenate([a, b, x - a - b], axis=0).astype(BF16)


def unstack3(y, n):
    return y[:n] + y[n : 2 * n] + y[2 * n : 3 * n]


def silu(v):
    return v / (1.0 + jnp.exp(-v))


def kernel(
    nx, ny, pos_h, spc_h, cnt_h, snd_h, edg_h, emb_c, emb_n, rad_w, env_w, lat_w, out_w, head_h,
    energy_ref, force_ref,
    pos_v, spc_v, cnt_v, snd_v, edg_v, embc_v, embn_v, rad_v, env_v, lat_v, out_v, head_v,
    feat_w, expand_w, env_cat, lat_cat, sca_cat, out_cat,
    tile_near, tile_own, got_near, got_own, got_edges,
    send_part, got_part, send_env, got_env, tile_tot, got_tot,
    hid_cat, hid, pre, harm_x,
    w_sem, near_s, near_r, own_s, own_r, part_s, part_r, env_s, env_r, tot_s, tot_r,
):
    gx, gy = lax.axis_index("gx"), lax.axis_index("gy")
    lx, ly = column(gx, gy)
    beside = [((lx + dx + nx) % nx, (ly + dy + ny) % ny) for dx, dy in AROUND]
    hosts = [host(*b) for b in beside]
    targets = [host((gx + dx + nx) % nx, (gy + dy + ny) % ny) for dx, dy in AROUND]

    barrier = pltpu.get_barrier_semaphore()
    for k in range(8):
        pl.semaphore_signal(barrier, inc=1, device_id=hosts[k], device_id_type=MESH)
    for k in range(9):
        pl.semaphore_signal(barrier, inc=1, device_id=beside[k], device_id_type=MESH)

    loads = [
        pltpu.make_async_copy(src, dst, w_sem.at[i])
        for i, (src, dst) in enumerate(
            (
                (pos_h, pos_v), (spc_h, spc_v), (cnt_h, cnt_v), (snd_h, snd_v), (edg_h, edg_v), (emb_c, embc_v),
                (emb_n, embn_v), (rad_w, rad_v), (env_w, env_v), (lat_w, lat_v), (out_w, out_v), (head_h, head_v),
            )
        )
    ]
    for load in loads:
        load.start()

    for load in loads[:5]:
        load.wait()
    lane = iota((1, 128), 1)
    spread_k = ((iota((8, 128), 1) - 32) // 4 == iota((8, 128), 0)) & (iota((8, 128), 1) >= 32)
    by_lane = mm(snd_v[0].astype(F32).astype(BF16), spread_k.astype(F32).astype(BF16))
    by_lane = jnp.where(iota((4, 128), 1) % 4 == iota((4, 128), 0), by_lane, 0.0)
    names = jnp.sum(by_lane, axis=0, keepdims=True)
    names = jnp.where(lane < 32, lane.astype(F32), jnp.where(lane < 64, names, -1.0))
    pick = (iota((32, 128), 0).astype(F32) == names).astype(F32)
    atoms = jnp.concatenate([pos_v[...], spc_v[...].astype(F32), jnp.zeros((4, 32), F32)], axis=0)
    picked = unstack3(mm(stack3(atoms), pick.astype(BF16)), 8)
    tile_near[...] = picked[:4]
    count_row = jnp.full((1, 128), cnt_v[0], jnp.int32).astype(F32)
    tile_own[...] = jnp.concatenate([picked[:4], names, count_row, names, names], axis=0)

    pl.semaphore_wait(barrier, 17)

    def remote(src, dst, send_sem, recv_sem, device):
        return pltpu.make_async_remote_copy(
            src_ref=src, dst_ref=dst, send_sem=send_sem, recv_sem=recv_sem, device_id=device, device_id_type=MESH
        )

    first = [
        remote(edg_v, got_edges, own_s.at[0], own_r.at[0], targets[8]),
        remote(tile_own, got_own, own_s.at[1], own_r.at[1], targets[8]),
    ]
    first += [remote(tile_near, got_near.at[k], near_s.at[k], near_r.at[k], targets[k]) for k in range(8)]
    for i in (2, 4, 7, 9, 3, 8, 0, 1, 5, 6):
        first[i].start()

    for load in loads[5:8]:
        load.wait()
    r, c, n = rad_v[...], embc_v[...], embn_v[...]
    feat_w[...] = jnp.concatenate(
        [top(r), r - top(r), top(r), top(c), c - top(c), top(n), n - top(n), jnp.zeros((72, 512), F32)], axis=0
    ).astype(BF16)
    row, col = iota((128, 640), 0), iota((128, 640), 1)
    expand_w[...] = ((row >= 64) & (row < 112) & (row % 16 == col // 64)).astype(F32).astype(BF16)
    loads[8].wait()
    for layer in range(2):
        e = 0.25 * env_v[layer]
        hi, lo = split(jnp.concatenate([e, e], axis=0).T)
        env_cat[layer, 0:512] = hi
        env_cat[layer, 512:1024] = hi
        env_cat[layer, 1024:1536] = lo
    loads[9].wait()

    def cut_latent(i, carry):
        layer, at = i // 8, pl.multiple_of((i % 8) * 64, 64)
        hi, lo = split(lat_v[layer, pl.ds(at, 64), :])
        lat_cat[layer, pl.ds(at, 64), :] = hi
        lat_cat[layer, pl.ds(pl.multiple_of(512 + at, 64), 64), :] = hi
        lat_cat[layer, pl.ds(pl.multiple_of(1024 + at, 64), 64), :] = lo
        return carry

    lax.fori_loop(0, 16, cut_latent, 0)
    for layer in range(2):
        for i, at in enumerate((576, 640, 512, 640)):
            hi, lo = split(lat_v[layer, at : at + 64, :])
            sca_cat[layer, 64 * i : 64 * i + 64] = hi
            sca_cat[layer, 256 + 64 * i : 320 + 64 * i] = hi
            sca_cat[layer, 512 + 64 * i : 576 + 64 * i] = lo
    loads[10].wait()
    for i in range(4):
        hi, lo = split(out_v[128 * i : 128 * i + 128, :].T)
        out_cat[0:512, 128 * i : 128 * i + 128] = hi
        out_cat[512:1024, 128 * i : 128 * i + 128] = hi
        out_cat[1024:1536, 128 * i : 128 * i + 128] = lo

    for copy in first:
        copy.wait_recv()

    own = got_own[...]
    pool = jnp.where(lane < 32, own[:4], 0.0)
    for k in range(8):
        pool = jnp.where((lane >= 32 + 4 * k) & (lane < 36 + 4 * k), got_near[k], pool)
    names = own[4:5]
    live = iota((1, 256), 1).astype(F32) < 8.0 * jnp.concatenate([own[5:6], own[5:6]], axis=1)
    ends = got_edges[0]
    ends = jnp.where(ends < 32, ends, 92 - ends + 2 * (ends & 3))
    ends = jnp.where(live, ends, -1)
    slot = iota((64, 256), 0)
    is_c = (slot == ends[0:1]).astype(F32)
    is_o = (slot == ends[1:2]).astype(F32)
    plus, minus = is_c + is_o, is_c - is_o
    coords = stack3(jnp.concatenate([pool, jnp.zeros((4, 128), F32)], axis=0)[:, :64])
    at_c = unstack3(mm(coords, is_c.astype(BF16)), 8)
    at_o = unstack3(mm(coords, is_o.astype(BF16)), 8)
    diff = at_o - at_c
    dx, dy, dz = diff[0:1], diff[1:2], diff[2:3]
    squared = dx * dx + dy * dy + dz * dz
    scale = 1.0 / jnp.sqrt(1.0 + squared)
    ux, uy, uz = dx * scale, dy * scale, dz * scale
    length = jnp.sqrt(squared)
    step = length - 0.5 * iota((8, 256), 0).astype(F32)
    basis = jnp.exp(-2.0 * step * step)
    kinds = iota((8, 256), 0).astype(F32)
    hot_c = (at_c[3:4] == kinds).astype(F32)
    hot_o = (at_o[3:4] == kinds).astype(F32)
    harm = jnp.concatenate(
        [
            jnp.ones_like(ux), ROOT3 * ux * uy, ROOT3 * uy * uz, 0.5 * (3.0 * uz * uz - 1.0), ROOT3 * ux * uz,
            0.5 * ROOT3 * (ux * ux - uy * uy), ux, uy, uz, jnp.zeros((7, 256), F32),
        ],
        axis=0,
    )
    h1 = top(harm)
    h2 = top(harm - h1)
    b1 = top(basis)
    feat = jnp.concatenate(
        [
            b1, b1, basis - b1, hot_c, hot_c, hot_o, hot_o, jnp.zeros((8, 256), F32),
            h1, h2, harm - h1 - h2, jnp.zeros((16, 256), F32),
        ],
        axis=0,
    ).T.astype(BF16)
    hid[...] = silu(mm(feat, feat_w[...]))
    harm_x[...] = mm(feat, expand_w[...])

    put_p = jnp.concatenate([plus, plus], axis=1).astype(BF16)
    put_m = jnp.concatenate([minus, minus], axis=1).astype(BF16)
    get_p = jnp.concatenate([plus, plus], axis=0).T.astype(BF16)
    get_m = jnp.concatenate([minus, minus], axis=0).T.astype(BF16)

    def keep_hidden():
        hi, lo = split(hid[...])
        hid_cat[:, 0:512] = hi
        hid_cat[:, 512:1024] = lo
        hid_cat[:, 1024:1536] = hi

    keep_hidden()
    same = None
    copies = []
    for layer in range(2):
        w = mm(hid_cat[...], env_cat[layer])
        contrib = jnp.concatenate([w] * 5, axis=1) * harm_x[...]
        hi, lo = split(contrib)
        both = jnp.concatenate([hi, lo], axis=0)
        part_p, part_m = mm(put_p, both[:, :384]), mm(put_m, both[:, 384:])
        part = jnp.concatenate([part_p, part_m], axis=1)
        for k in range(8):
            send_part[layer, k] = part[32 + 4 * k : 36 + 4 * k]
        back = [
            remote(
                send_part.at[layer, k], got_part.at[layer, k], part_s.at[layer, k], part_r.at[layer, k], hosts[7 - k]
            )
            for k in range(8)
        ]
        for k in ORDER:
            back[k].start()
        copies += back
        if same is None:
            names_col = own.T[:, 4:5]
            same = (names_col[:64] == names).astype(F32)[:, :64]
            same = jnp.concatenate([same, same], axis=1).astype(BF16)
        pre[...] = mm(hid_cat[...], lat_cat[layer])
        for copy in back:
            copy.wait_recv()
        got = got_part[layer].reshape(32, 640)
        hi, lo = split(jnp.concatenate([part[:32], got], axis=0))
        env = mm(same, jnp.concatenate([hi, lo], axis=0))
        for k in range(8):
            send_env[layer, k] = env[32 + 4 * k : 36 + 4 * k]
        forth = [
            remote(send_env.at[layer, k], got_env.at[layer, k], env_s.at[layer, k], env_r.at[layer, k], hosts[k])
            for k in range(8)
        ]
        for k in ORDER:
            forth[k].start()
        copies += forth
        for copy in forth:
            copy.wait_recv()
        got = got_env[layer].reshape(32, 640)
        hi, lo = split(jnp.concatenate([env[:32], got], axis=0))
        both = jnp.concatenate([hi, lo], axis=0)
        prod = jnp.concatenate([mm(get_p, both[:, :384]), mm(get_m, both[:, 384:])], axis=1) * harm_x[...]
        t0, t1, t2, t3, t4 = [prod[:, 128 * i : 128 * i + 128] for i in range(5)]
        t12 = t1 + t2
        low = iota((256, 128), 1) < 64
        fold = jnp.where(low, t3 + pltpu.roll(t3, 64, 1) + t4, t12 + pltpu.roll(t12, 64, 1))
        hi, lo = split(jnp.concatenate([fold, t0], axis=1))
        hid[...] += silu(pre[...] + mm(jnp.concatenate([hi, lo, hi], axis=1), sca_cat[layer]))
        keep_hidden()

    hi, lo = split(silu(mm(hid_cat[...], out_cat[...])))
    loads[11].wait()
    h = head_v[...]
    hh = top(h)
    hw = jnp.concatenate([hh, h - hh, jnp.zeros((4, 512), F32)], axis=0).astype(BF16)
    by_hi, by_lo = mm_nt(hw, hi), mm_nt(hw, lo)
    heads = by_hi[0:2] + by_hi[2:4] + by_lo[0:2]
    push = heads[1:2]
    vals = jnp.concatenate([0.5 * heads[0:1], push * ux, push * uy, push * uz, jnp.zeros((4, 256), F32)], axis=0)
    vals = stack3(vals)
    tot_p, tot_m = unstack3(mm(vals, get_p), 8), unstack3(mm(vals, get_m), 8)
    tile_tot[...] = jnp.where(iota((4, 128), 0) == 0, tot_p[:4], tot_m[:4])
    last = [remote(tile_tot, got_tot.at[k], tot_s.at[k], tot_r.at[k], beside[7 - k]) for k in range(8)]
    last.append(remote(tile_tot, got_tot.at[8], tot_s.at[8], tot_r.at[8], beside[8]))
    for copy in last:
        copy.start()
    for copy in first + copies:
        copy.wait_send()
    for copy in last:
        copy.wait_recv()
    total = jnp.where(lane < 32, got_tot[8], 0.0)
    for k in range(8):
        total = jnp.where((lane >= 32 + 4 * k) & (lane < 36 + 4 * k), got_tot[k], total)
    total = stack3(jnp.concatenate([total, jnp.zeros((4, 128), F32)], axis=0))
    out = unstack3(mm_nt(total, pick.astype(BF16)), 8)
    energy_ref[...] = out[0:1]
    force_ref[...] = out[1:4]
    for copy in last:
        copy.wait_send()


def solution(mesh):
    nx, ny = mesh.shape["gx"], mesh.shape["gy"]

    def local(
        positions, species, atom_count, send_list, edges, centre_embed, neighbour_embed, radial_weight, env_weight,
        latent_weight, out_weight, head_weight,
    ):
        vmem, anywhere = pl.BlockSpec(memory_space=pltpu.VMEM), pl.BlockSpec(memory_space=pl.ANY)
        dma = pltpu.SemaphoreType.DMA
        energy, forces = pl.pallas_call(
            functools.partial(kernel, nx, ny),
            out_shape=(jax.ShapeDtypeStruct((1, 32), F32), jax.ShapeDtypeStruct((3, 32), F32)),
            in_specs=[anywhere] * 12,
            out_specs=(vmem, vmem),
            scratch_shapes=[
                pltpu.VMEM((3, 32), F32), pltpu.VMEM((1, 32), jnp.int32), pltpu.SMEM((1,), jnp.int32),
                pltpu.VMEM((1, 4, 8), jnp.int32), pltpu.VMEM((1, 2, 256), jnp.int32),
                pltpu.VMEM((8, 512), F32), pltpu.VMEM((8, 512), F32), pltpu.VMEM((8, 512), F32),
                pltpu.VMEM((2, 64, 512), F32), pltpu.VMEM((2, 704, 512), F32), pltpu.VMEM((512, 512), F32),
                pltpu.VMEM((2, 512), F32), pltpu.VMEM((128, 512), BF16), pltpu.VMEM((128, 640), BF16), pltpu.VMEM((2, 1536, 128), BF16),
                pltpu.VMEM((2, 1536, 512), BF16), pltpu.VMEM((2, 768, 512), BF16), pltpu.VMEM((1536, 512), BF16),
                pltpu.VMEM((4, 128), F32), pltpu.VMEM((8, 128), F32), pltpu.VMEM((8, 4, 128), F32),
                pltpu.VMEM((8, 128), F32), pltpu.VMEM((1, 2, 256), jnp.int32),
                pltpu.VMEM((2, 8, 4, 640), F32), pltpu.VMEM((2, 8, 4, 640), F32),
                pltpu.VMEM((2, 8, 4, 640), F32), pltpu.VMEM((2, 8, 4, 640), F32),
                pltpu.VMEM((4, 128), F32), pltpu.VMEM((9, 4, 128), F32),
                pltpu.VMEM((256, 1536), BF16), pltpu.VMEM((256, 512), F32), pltpu.VMEM((256, 512), F32),
                pltpu.VMEM((256, 640), F32),
                dma((12,)), dma((8,)), dma((8,)), dma((2,)), dma((2,)), dma((2, 8)), dma((2, 8)), dma((2, 8)),
                dma((2, 8)), dma((9,)), dma((9,)),
            ],
            compiler_params=pltpu.CompilerParams(
                collective_id=0, has_side_effects=True, vmem_limit_bytes=64 * 1024 * 1024
            ),
            name="pair_network",
        )(
            positions, species.reshape(1, -1), atom_count, send_list.transpose(0, 2, 1), edges,
            centre_embed.T, neighbour_embed.T, radial_weight.T, env_weight, latent_weight.transpose(0, 2, 1),
            out_weight, head_weight,
        )
        return energy.reshape(-1), forces

    placed = (
        P(None, ("gx", "gy")), P(("gx", "gy")), P(("gx", "gy")), P(("gx", "gy"), None, None),
        P(("gx", "gy"), None, None), P(), P(), P(), P(), P(), P(), P(),
    )
    return jax.shard_map(
        local, mesh=mesh, in_specs=placed, out_specs=(P(("gx", "gy")), P(None, ("gx", "gy"))), check_vma=False
    )
```

```python
import functools

import jax
import jax.numpy as jnp
from jax import lax
from jax.experimental import pallas as pl
from jax.experimental.pallas import tpu as pltpu
from jax.sharding import PartitionSpec as P

MESH = pl.DeviceIdType.MESH
F32 = jnp.float32
BF16 = jnp.bfloat16
OFFSETS = ((-1, -1), (-1, 0), (-1, 1), (0, -1), (0, 1), (1, -1), (1, 0), (1, 1))
AROUND = OFFSETS + ((0, 0),)
ORDER = (0, 2, 5, 7, 1, 6, 3, 4)
ROOT3 = 3.0 ** 0.5


def host(lx, ly):
    a, b = (lx + 8) % 64, (ly + 2) % 16
    zi, yy, t = a // 8, a % 8, b // 2
    x = t // 2
    z = 2 * zi + (t + x) % 2
    y = yy + (zi % 2) * (7 - 2 * yy)
    return (z % 8) * 8 + y, x * 4 + (z // 8) * 2 + b % 2


def column(gx, gy):
    y, x = gx % 8, gy // 4
    z = ((gy // 2) % 2) * 8 + gx // 8
    zi = z // 2
    a = 8 * zi + y + (zi % 2) * (7 - 2 * y)
    b = 4 * x + 2 * ((z + x) % 2) + gy % 2
    return (a + 56) % 64, (b + 14) % 16


def iota(shape, dim):
    return lax.broadcasted_iota(jnp.int32, shape, dim)


def mm(a, b):
    return lax.dot_general(a, b, (((1,), (0,)), ((), ())), preferred_element_type=F32)


def mm_nt(a, b):
    return lax.dot_general(a, b, (((1,), (1,)), ((), ())), preferred_element_type=F32)


def top(x):
    return x.astype(BF16).astype(F32)


def split(x):
    hi = x.astype(BF16)
    return hi, (x - hi.astype(F32)).astype(BF16)


def stack3(x):
    a = top(x)
    b = top(x - a)
    return jnp.concatenate([a, b, x - a - b], axis=0).astype(BF16)


def unstack3(y, n):
    return y[:n] + y[n : 2 * n] + y[2 * n : 3 * n]


def silu(v):
    return v / (1.0 + jnp.exp(-v))


def picked_names(snd_v):
    lane = iota((1, 128), 1)
    spread_k = ((iota((8, 128), 1) - 32) // 4 == iota((8, 128), 0)) & (iota((8, 128), 1) >= 32)
    by_lane = mm(snd_v[0].astype(F32).astype(BF16), spread_k.astype(F32).astype(BF16))
    by_lane = jnp.where(iota((4, 128), 1) % 4 == iota((4, 128), 0), by_lane, 0.0)
    names = jnp.sum(by_lane, axis=0, keepdims=True)
    names = jnp.where(lane < 32, lane.astype(F32), jnp.where(lane < 64, names, -1.0))
    return names


def kernel(
    nx, ny, pos_h, spc_h, cnt_h, snd_h, edg_h, emb_c, emb_n, rad_w, env_w, lat_w, out_w, head_h,
    got_tot, names_h,
    pos_v, spc_v, cnt_v, snd_v, edg_v, embc_v, embn_v, rad_v, env_v, lat_v, out_v, head_v,
    feat_w, expand_w, env_cat, lat_cat, sca_cat, out_cat,
    tile_near, tile_own, got_near, got_own, got_edges,
    send_part, got_part, send_env, got_env, tile_tot,
    hid_cat, hid, pre, harm_x,
    w_sem, near_s, near_r, own_s, own_r, part_s, part_r, env_s, env_r, tot_s, tot_r, name_sem,
):
    gx, gy = lax.axis_index("gx"), lax.axis_index("gy")
    lx, ly = column(gx, gy)
    beside = [((lx + dx + nx) % nx, (ly + dy + ny) % ny) for dx, dy in AROUND]
    hosts = [host(*b) for b in beside]
    targets = [host((gx + dx + nx) % nx, (gy + dy + ny) % ny) for dx, dy in AROUND]

    barrier = pltpu.get_barrier_semaphore()
    for k in (0, 2, 5, 7, 1, 6, 3, 4, 8):
        pl.semaphore_signal(barrier, inc=1, device_id=beside[k], device_id_type=MESH)

    loads = [
        pltpu.make_async_copy(src, dst, w_sem.at[i])
        for i, (src, dst) in enumerate(
            (
                (pos_h, pos_v), (spc_h, spc_v), (cnt_h, cnt_v), (snd_h, snd_v), (edg_h, edg_v), (emb_c, embc_v),
                (emb_n, embn_v), (rad_w, rad_v), (env_w, env_v), (lat_w, lat_v), (out_w, out_v), (head_h, head_v),
            )
        )
    ]
    for load in loads:
        load.start()

    for load in loads[:5]:
        load.wait()
    lane = iota((1, 128), 1)
    names = picked_names(snd_v)
    pick = (iota((32, 128), 0).astype(F32) == names).astype(F32)
    atoms = jnp.concatenate([pos_v[...], spc_v[...].astype(F32), jnp.zeros((4, 32), F32)], axis=0)
    picked = unstack3(mm(stack3(atoms), pick.astype(BF16)), 8)
    tile_near[...] = picked[:4]
    count_row = jnp.full((1, 128), cnt_v[0], jnp.int32).astype(F32)
    tile_own[...] = jnp.concatenate([picked[:4], names, count_row, names, names], axis=0)
    keep_names = pltpu.make_async_copy(tile_own, names_h, name_sem.at[0])
    keep_names.start()

    pl.semaphore_wait(barrier, 9)

    def remote(src, dst, send_sem, recv_sem, device):
        return pltpu.make_async_remote_copy(
            src_ref=src, dst_ref=dst, send_sem=send_sem, recv_sem=recv_sem, device_id=device, device_id_type=MESH
        )

    first = [
        remote(edg_v, got_edges, own_s.at[0], own_r.at[0], targets[8]),
        remote(tile_own, got_own, own_s.at[1], own_r.at[1], targets[8]),
    ]
    first += [remote(tile_near, got_near.at[k], near_s.at[k], near_r.at[k], targets[k]) for k in range(8)]
    for i in (2, 4, 7, 9, 3, 8, 0, 1, 5, 6):
        first[i].start()

    for load in loads[5:8]:
        load.wait()
    r, c, n = rad_v[...], embc_v[...], embn_v[...]
    feat_w[...] = jnp.concatenate(
        [top(r), r - top(r), top(r), top(c), c - top(c), top(n), n - top(n), jnp.zeros((72, 512), F32)], axis=0
    ).astype(BF16)
    row, col = iota((128, 640), 0), iota((128, 640), 1)
    expand_w[...] = ((row >= 64) & (row < 112) & (row % 16 == col // 64)).astype(F32).astype(BF16)
    loads[8].wait()
    for layer in range(2):
        e = 0.25 * env_v[layer]
        hi, lo = split(jnp.concatenate([e, e], axis=0).T)
        env_cat[layer, 0:512] = hi
        env_cat[layer, 512:1024] = hi
        env_cat[layer, 1024:1536] = lo
    loads[9].wait()

    def cut_latent(i, carry):
        layer, at = i // 8, pl.multiple_of((i % 8) * 64, 64)
        hi, lo = split(lat_v[layer, pl.ds(at, 64), :])
        lat_cat[layer, pl.ds(at, 64), :] = hi
        lat_cat[layer, pl.ds(pl.multiple_of(512 + at, 64), 64), :] = hi
        lat_cat[layer, pl.ds(pl.multiple_of(1024 + at, 64), 64), :] = lo
        return carry

    lax.fori_loop(0, 16, cut_latent, 0)
    for layer in range(2):
        for i, at in enumerate((576, 640, 512, 640)):
            hi, lo = split(lat_v[layer, at : at + 64, :])
            sca_cat[layer, 64 * i : 64 * i + 64] = hi
            sca_cat[layer, 256 + 64 * i : 320 + 64 * i] = hi
            sca_cat[layer, 512 + 64 * i : 576 + 64 * i] = lo
    loads[10].wait()
    for i in range(4):
        hi, lo = split(out_v[128 * i : 128 * i + 128, :].T)
        out_cat[0:512, 128 * i : 128 * i + 128] = hi
        out_cat[512:1024, 128 * i : 128 * i + 128] = hi
        out_cat[1024:1536, 128 * i : 128 * i + 128] = lo

    for copy in first:
        copy.wait_recv()

    own = got_own[...]
    pool = jnp.where(lane < 32, own[:4], 0.0)
    for k in range(8):
        pool = jnp.where((lane >= 32 + 4 * k) & (lane < 36 + 4 * k), got_near[k], pool)
    names = own[4:5]
    live = iota((1, 256), 1).astype(F32) < 8.0 * jnp.concatenate([own[5:6], own[5:6]], axis=1)
    ends = got_edges[0]
    ends = jnp.where(ends < 32, ends, 92 - ends + 2 * (ends & 3))
    ends = jnp.where(live, ends, -1)
    slot = iota((64, 256), 0)
    is_c = (slot == ends[0:1]).astype(F32)
    is_o = (slot == ends[1:2]).astype(F32)
    plus, minus = is_c + is_o, is_c - is_o
    coords = stack3(jnp.concatenate([pool, jnp.zeros((4, 128), F32)], axis=0)[:, :64])
    at_c = unstack3(mm(coords, is_c.astype(BF16)), 8)
    at_o = unstack3(mm(coords, is_o.astype(BF16)), 8)
    diff = at_o - at_c
    dx, dy, dz = diff[0:1], diff[1:2], diff[2:3]
    squared = dx * dx + dy * dy + dz * dz
    scale = 1.0 / jnp.sqrt(1.0 + squared)
    ux, uy, uz = dx * scale, dy * scale, dz * scale
    length = jnp.sqrt(squared)
    step = length - 0.5 * iota((8, 256), 0).astype(F32)
    basis = jnp.exp(-2.0 * step * step)
    kinds = iota((8, 256), 0).astype(F32)
    hot_c = (at_c[3:4] == kinds).astype(F32)
    hot_o = (at_o[3:4] == kinds).astype(F32)
    harm = jnp.concatenate(
        [
            jnp.ones_like(ux), ROOT3 * ux * uy, ROOT3 * uy * uz, 0.5 * (3.0 * uz * uz - 1.0), ROOT3 * ux * uz,
            0.5 * ROOT3 * (ux * ux - uy * uy), ux, uy, uz, jnp.zeros((7, 256), F32),
        ],
        axis=0,
    )
    h1 = top(harm)
    h2 = top(harm - h1)
    b1 = top(basis)
    feat = jnp.concatenate(
        [
            b1, b1, basis - b1, hot_c, hot_c, hot_o, hot_o, jnp.zeros((8, 256), F32),
            h1, h2, harm - h1 - h2, jnp.zeros((16, 256), F32),
        ],
        axis=0,
    ).T.astype(BF16)
    hid[...] = silu(mm(feat, feat_w[...]))
    harm_x[...] = mm(feat, expand_w[...])

    put_p = jnp.concatenate([plus, plus], axis=1).astype(BF16)
    put_m = jnp.concatenate([minus, minus], axis=1).astype(BF16)

    def keep_hidden():
        hi, lo = split(hid[...])
        hid_cat[:, 0:512] = hi
        hid_cat[:, 512:1024] = lo
        hid_cat[:, 1024:1536] = hi

    keep_hidden()
    same = None
    copies = []
    for layer in range(2):
        w = mm(hid_cat[...], env_cat[layer])
        contrib = jnp.concatenate([w] * 5, axis=1) * harm_x[...]
        hi, lo = split(contrib)
        both = jnp.concatenate([hi, lo], axis=0)
        part_p, part_m = mm(put_p, both[:, :384]), mm(put_m, both[:, 384:])
        part = jnp.concatenate([part_p, part_m], axis=1)
        for k in range(8):
            send_part[layer, k] = part[32 + 4 * k : 36 + 4 * k]
        back = [
            remote(
                send_part.at[layer, k], got_part.at[layer, k], part_s.at[layer, k], part_r.at[layer, k], hosts[7 - k]
            )
            for k in range(8)
        ]
        for k in ORDER:
            back[k].start()
        copies += back
        if same is None:
            names_col = own.T[:, 4:5]
            same = (names_col[:64] == names).astype(F32)[:, :64]
            same = jnp.concatenate([same, same], axis=1).astype(BF16)
            get_p = jnp.concatenate([plus, plus], axis=0).T.astype(BF16)
            get_m = jnp.concatenate([minus, minus], axis=0).T.astype(BF16)
        pre[...] = mm(hid_cat[...], lat_cat[layer])
        for copy in back:
            copy.wait_recv()
        got = got_part[layer].reshape(32, 640)
        hi, lo = split(jnp.concatenate([part[:32], got], axis=0))
        env = mm(same, jnp.concatenate([hi, lo], axis=0))
        for k in range(8):
            send_env[layer, k] = env[32 + 4 * k : 36 + 4 * k]
        forth = [
            remote(send_env.at[layer, k], got_env.at[layer, k], env_s.at[layer, k], env_r.at[layer, k], hosts[k])
            for k in range(8)
        ]
        for k in ORDER:
            forth[k].start()
        copies += forth
        for copy in forth:
            copy.wait_recv()
        got = got_env[layer].reshape(32, 640)
        hi, lo = split(jnp.concatenate([env[:32], got], axis=0))
        both = jnp.concatenate([hi, lo], axis=0)
        prod = jnp.concatenate([mm(get_p, both[:, :384]), mm(get_m, both[:, 384:])], axis=1) * harm_x[...]
        t0, t1, t2, t3, t4 = [prod[:, 128 * i : 128 * i + 128] for i in range(5)]
        t12 = t1 + t2
        low = iota((256, 128), 1) < 64
        fold = jnp.where(low, t3 + pltpu.roll(t3, 64, 1) + t4, t12 + pltpu.roll(t12, 64, 1))
        hi, lo = split(jnp.concatenate([fold, t0], axis=1))
        hid[...] += silu(pre[...] + mm(jnp.concatenate([hi, lo, hi], axis=1), sca_cat[layer]))
        keep_hidden()

    hi, lo = split(silu(mm(hid_cat[...], out_cat[...])))
    loads[11].wait()
    h = head_v[...]
    hh = top(h)
    hw = jnp.concatenate([hh, h - hh, jnp.zeros((4, 512), F32)], axis=0).astype(BF16)
    by_hi, by_lo = mm_nt(hw, hi), mm_nt(hw, lo)
    heads = by_hi[0:2] + by_hi[2:4] + by_lo[0:2]
    push = heads[1:2]
    vals = jnp.concatenate([0.5 * heads[0:1], push * ux, push * uy, push * uz, jnp.zeros((4, 256), F32)], axis=0)
    vals = stack3(vals)
    tot_p, tot_m = unstack3(mm(vals, get_p), 8), unstack3(mm(vals, get_m), 8)
    tile_tot[...] = jnp.where(iota((4, 128), 0) == 0, tot_p[:4], tot_m[:4])
    last = [remote(tile_tot, got_tot.at[k], tot_s.at[k], tot_r.at[k], beside[7 - k]) for k in range(8)]
    last.append(remote(tile_tot, got_tot.at[8], tot_s.at[8], tot_r.at[8], beside[8]))
    for copy in last:
        copy.start()
    for copy in first + copies:
        copy.wait_send()
    keep_names.wait()
    for copy in last:
        copy.wait_recv()
    for copy in last:
        copy.wait_send()


def owner_kernel(tot_h, names_h, energy_h, force_h, tot_v, names_v, energy_v, force_v, sem):
    loads = [pltpu.make_async_copy(tot_h, tot_v, sem.at[0]), pltpu.make_async_copy(names_h, names_v, sem.at[1])]
    for load in loads:
        load.start()
    for load in loads:
        load.wait()
    lane = iota((1, 128), 1)
    pick = (iota((32, 128), 0).astype(F32) == names_v[4:5]).astype(F32)
    total = jnp.where(lane < 32, tot_v[8], 0.0)
    for k in range(8):
        total = jnp.where((lane >= 32 + 4 * k) & (lane < 36 + 4 * k), tot_v[k], total)
    total = stack3(jnp.concatenate([total, jnp.zeros((4, 128), F32)], axis=0))
    out = unstack3(mm_nt(total, pick.astype(BF16)), 8)
    energy_v[...] = out[0:1]
    force_v[...] = out[1:4]
    stores = [pltpu.make_async_copy(energy_v, energy_h, sem.at[2]), pltpu.make_async_copy(force_v, force_h, sem.at[3])]
    for store in stores:
        store.start()
    for store in stores:
        store.wait()


def solution(mesh):
    nx, ny = mesh.shape["gx"], mesh.shape["gy"]

    def local(
        positions, species, atom_count, send_list, edges, centre_embed, neighbour_embed, radial_weight, env_weight,
        latent_weight, out_weight, head_weight,
    ):
        anywhere = pl.BlockSpec(memory_space=pl.ANY)
        dma = pltpu.SemaphoreType.DMA
        totals, names = pl.pallas_call(
            functools.partial(kernel, nx, ny),
            out_shape=(jax.ShapeDtypeStruct((9, 4, 128), F32), jax.ShapeDtypeStruct((8, 128), F32)),
            in_specs=[anywhere] * 12,
            out_specs=(anywhere, anywhere),
            scratch_shapes=[
                pltpu.VMEM((3, 32), F32), pltpu.VMEM((1, 32), jnp.int32), pltpu.SMEM((1,), jnp.int32),
                pltpu.VMEM((1, 4, 8), jnp.int32), pltpu.VMEM((1, 2, 256), jnp.int32),
                pltpu.VMEM((8, 512), F32), pltpu.VMEM((8, 512), F32), pltpu.VMEM((8, 512), F32),
                pltpu.VMEM((2, 64, 512), F32), pltpu.VMEM((2, 704, 512), F32), pltpu.VMEM((512, 512), F32),
                pltpu.VMEM((2, 512), F32), pltpu.VMEM((128, 512), BF16), pltpu.VMEM((128, 640), BF16), pltpu.VMEM((2, 1536, 128), BF16),
                pltpu.VMEM((2, 1536, 512), BF16), pltpu.VMEM((2, 768, 512), BF16), pltpu.VMEM((1536, 512), BF16),
                pltpu.VMEM((4, 128), F32), pltpu.VMEM((8, 128), F32), pltpu.VMEM((8, 4, 128), F32),
                pltpu.VMEM((8, 128), F32), pltpu.VMEM((1, 2, 256), jnp.int32),
                pltpu.VMEM((2, 8, 4, 640), F32), pltpu.VMEM((2, 8, 4, 640), F32),
                pltpu.VMEM((2, 8, 4, 640), F32), pltpu.VMEM((2, 8, 4, 640), F32),
                pltpu.VMEM((4, 128), F32),
                pltpu.VMEM((256, 1536), BF16), pltpu.VMEM((256, 512), F32), pltpu.VMEM((256, 512), F32),
                pltpu.VMEM((256, 640), F32),
                dma((12,)), dma((8,)), dma((8,)), dma((2,)), dma((2,)), dma((2, 8)), dma((2, 8)), dma((2, 8)),
                dma((2, 8)), dma((9,)), dma((9,)), dma((1,)),
            ],
            compiler_params=pltpu.CompilerParams(
                collective_id=0, has_side_effects=True, vmem_limit_bytes=64 * 1024 * 1024
            ),
            name="pair_network",
        )(
            positions, species.reshape(1, -1), atom_count, send_list.transpose(0, 2, 1), edges,
            centre_embed.T, neighbour_embed.T, radial_weight.T, env_weight, latent_weight.transpose(0, 2, 1),
            out_weight, head_weight,
        )
        energy, forces = pl.pallas_call(
            owner_kernel,
            out_shape=(jax.ShapeDtypeStruct((1, 32), F32), jax.ShapeDtypeStruct((3, 32), F32)),
            in_specs=[anywhere] * 2,
            out_specs=(anywhere, anywhere),
            scratch_shapes=[
                pltpu.VMEM((9, 4, 128), F32), pltpu.VMEM((8, 128), F32), pltpu.VMEM((1, 32), F32),
                pltpu.VMEM((3, 32), F32), dma((4,)),
            ],
            compiler_params=pltpu.CompilerParams(vmem_limit_bytes=64 * 1024 * 1024),
            name="owner_sums",
        )(totals, names)
        return energy.reshape(-1), forces

    placed = (
        P(None, ("gx", "gy")), P(("gx", "gy")), P(("gx", "gy")), P(("gx", "gy"), None, None),
        P(("gx", "gy"), None, None), P(), P(), P(), P(), P(), P(), P(),
    )
    return jax.shard_map(
        local, mesh=mesh, in_specs=placed, out_specs=(P(("gx", "gy")), P(None, ("gx", "gy"))), check_vma=False
    )
```

```python
import functools

import jax
import jax.numpy as jnp
from jax import lax
from jax.experimental import pallas as pl
from jax.experimental.pallas import tpu as pltpu
from jax.sharding import PartitionSpec as P

MESH = pl.DeviceIdType.MESH
F32 = jnp.float32
BF16 = jnp.bfloat16
OFFSETS = ((-1, -1), (-1, 0), (-1, 1), (0, -1), (0, 1), (1, -1), (1, 0), (1, 1))
AROUND = OFFSETS + ((0, 0),)
ORDER = (0, 2, 5, 7, 1, 6, 3, 4)
ROOT3 = 3.0 ** 0.5


def host(lx, ly):
    a, b = (lx + 46) % 64, (ly + 2) % 16
    zi, yy, t = a // 8, a % 8, b // 2
    x = t // 2
    z = (2 * zi + (t + x) % 2 + 6) % 16
    y = (yy + (zi % 2) * (7 - 2 * yy) + 3) % 8
    return (z % 8) * 8 + y, x * 4 + (z // 8) * 2 + b % 2


def column(gx, gy):
    y, x = (gx % 8 + 5) % 8, gy // 4
    z = (((gy // 2) % 2) * 8 + gx // 8 + 10) % 16
    zi = z // 2
    a = 8 * zi + y + (zi % 2) * (7 - 2 * y)
    b = 4 * x + 2 * ((z + x) % 2) + gy % 2
    return (a + 18) % 64, (b + 14) % 16


def iota(shape, dim):
    return lax.broadcasted_iota(jnp.int32, shape, dim)


def mm(a, b):
    return lax.dot_general(a, b, (((1,), (0,)), ((), ())), preferred_element_type=F32)


def mm_nt(a, b):
    return lax.dot_general(a, b, (((1,), (1,)), ((), ())), preferred_element_type=F32)


def top(x):
    return x.astype(BF16).astype(F32)


def split(x):
    hi = x.astype(BF16)
    return hi, (x - hi.astype(F32)).astype(BF16)


def stack3(x):
    a = top(x)
    b = top(x - a)
    return jnp.concatenate([a, b, x - a - b], axis=0).astype(BF16)


def unstack3(y, n):
    return y[:n] + y[n : 2 * n] + y[2 * n : 3 * n]


def silu(v):
    return v / (1.0 + jnp.exp(-v))


def picked_names(snd_v):
    lane = iota((1, 128), 1)
    spread_k = ((iota((8, 128), 1) - 32) // 4 == iota((8, 128), 0)) & (iota((8, 128), 1) >= 32)
    by_lane = mm(snd_v[0].astype(F32).astype(BF16), spread_k.astype(F32).astype(BF16))
    by_lane = jnp.where(iota((4, 128), 1) % 4 == iota((4, 128), 0), by_lane, 0.0)
    names = jnp.sum(by_lane, axis=0, keepdims=True)
    names = jnp.where(lane < 32, lane.astype(F32), jnp.where(lane < 64, names, -1.0))
    return names


def kernel(
    nx, ny, pos_h, spc_h, cnt_h, snd_h, edg_h, emb_c, emb_n, rad_w, env_w, lat_w, out_w, head_h,
    got_tot, names_h,
    pos_v, spc_v, cnt_v, snd_v, edg_v, embc_v, embn_v, rad_v, env_v, lat_v, out_v, head_v,
    feat_w, expand_w, env_cat, lat_cat, sca_cat, out_cat,
    tile_near, tile_own, got_near, got_own, got_edges,
    send_part, got_part, send_env, got_env, tile_tot,
    hid_cat, hid, pre, harm_x,
    w_sem, near_s, near_r, own_s, own_r, part_s, part_r, env_s, env_r, tot_s, tot_r, name_sem,
):
    gx, gy = lax.axis_index("gx"), lax.axis_index("gy")
    lx, ly = column(gx, gy)
    beside = [((lx + dx + nx) % nx, (ly + dy + ny) % ny) for dx, dy in AROUND]
    hosts = [host(*b) for b in beside]
    targets = [host((gx + dx + nx) % nx, (gy + dy + ny) % ny) for dx, dy in AROUND]

    loads = [
        pltpu.make_async_copy(src, dst, w_sem.at[i])
        for i, (src, dst) in enumerate(
            (
                (pos_h, pos_v), (spc_h, spc_v), (cnt_h, cnt_v), (snd_h, snd_v), (edg_h, edg_v), (emb_c, embc_v),
                (emb_n, embn_v), (rad_w, rad_v), (env_w, env_v), (lat_w, lat_v), (out_w, out_v), (head_h, head_v),
            )
        )
    ]
    for load in loads[:5]:
        load.start()

    barrier = pltpu.get_barrier_semaphore()
    for k in (0, 2, 5, 7, 1, 6, 3, 4, 8):
        pl.semaphore_signal(barrier, inc=1, device_id=beside[k], device_id_type=MESH)
    for load in loads[5:]:
        load.start()

    for load in loads[:5]:
        load.wait()
    lane = iota((1, 128), 1)
    names = picked_names(snd_v)
    pick = (iota((32, 128), 0).astype(F32) == names).astype(F32)
    atoms = jnp.concatenate([pos_v[...], spc_v[...].astype(F32), jnp.zeros((4, 32), F32)], axis=0)
    picked = unstack3(mm(stack3(atoms), pick.astype(BF16)), 8)
    tile_near[...] = picked[:4]
    count_row = jnp.full((1, 128), cnt_v[0], jnp.int32).astype(F32)
    tile_own[...] = jnp.concatenate([picked[:4], names, count_row, names, names], axis=0)
    keep_names = pltpu.make_async_copy(tile_own, names_h, name_sem.at[0])
    keep_names.start()

    pl.semaphore_wait(barrier, 9)

    def remote(src, dst, send_sem, recv_sem, device):
        return pltpu.make_async_remote_copy(
            src_ref=src, dst_ref=dst, send_sem=send_sem, recv_sem=recv_sem, device_id=device, device_id_type=MESH
        )

    first = [
        remote(edg_v, got_edges, own_s.at[0], own_r.at[0], targets[8]),
        remote(tile_own, got_own, own_s.at[1], own_r.at[1], targets[8]),
    ]
    first += [remote(tile_near, got_near.at[k], near_s.at[k], near_r.at[k], targets[k]) for k in range(8)]
    for i in (2, 4, 7, 9, 3, 8, 0, 1, 5, 6):
        first[i].start()

    for load in loads[5:8]:
        load.wait()
    r, c, n = rad_v[...], embc_v[...], embn_v[...]
    feat_w[...] = jnp.concatenate(
        [top(r), r - top(r), top(r), top(c), c - top(c), top(n), n - top(n), jnp.zeros((72, 512), F32)], axis=0
    ).astype(BF16)
    row, col = iota((128, 640), 0), iota((128, 640), 1)
    expand_w[...] = ((row >= 64) & (row < 112) & (row % 16 == col // 64)).astype(F32).astype(BF16)
    loads[8].wait()
    for layer in range(2):
        e = 0.25 * env_v[layer]
        hi, lo = split(jnp.concatenate([e, e], axis=0).T)
        env_cat[layer, 0:512] = hi
        env_cat[layer, 512:1024] = hi
        env_cat[layer, 1024:1536] = lo
    loads[9].wait()

    def cut_latent(i, carry):
        layer, at = i // 8, pl.multiple_of((i % 8) * 64, 64)
        hi, lo = split(lat_v[layer, pl.ds(at, 64), :])
        lat_cat[layer, pl.ds(at, 64), :] = hi
        lat_cat[layer, pl.ds(pl.multiple_of(512 + at, 64), 64), :] = hi
        lat_cat[layer, pl.ds(pl.multiple_of(1024 + at, 64), 64), :] = lo
        return carry

    lax.fori_loop(0, 16, cut_latent, 0)
    for layer in range(2):
        for i, at in enumerate((576, 640, 512, 640)):
            hi, lo = split(lat_v[layer, at : at + 64, :])
            sca_cat[layer, 64 * i : 64 * i + 64] = hi
            sca_cat[layer, 256 + 64 * i : 320 + 64 * i] = hi
            sca_cat[layer, 512 + 64 * i : 576 + 64 * i] = lo
    loads[10].wait()
    for i in range(4):
        hi, lo = split(out_v[128 * i : 128 * i + 128, :].T)
        out_cat[0:512, 128 * i : 128 * i + 128] = hi
        out_cat[512:1024, 128 * i : 128 * i + 128] = hi
        out_cat[1024:1536, 128 * i : 128 * i + 128] = lo

    for copy in first:
        copy.wait_recv()

    own = got_own[...]
    pool = jnp.where(lane < 32, own[:4], 0.0)
    for k in range(8):
        pool = jnp.where((lane >= 32 + 4 * k) & (lane < 36 + 4 * k), got_near[k], pool)
    names = own[4:5]
    live = iota((1, 256), 1).astype(F32) < 8.0 * jnp.concatenate([own[5:6], own[5:6]], axis=1)
    ends = got_edges[0]
    ends = jnp.where(ends < 32, ends, 92 - ends + 2 * (ends & 3))
    ends = jnp.where(live, ends, -1)
    slot = iota((64, 256), 0)
    is_c = (slot == ends[0:1]).astype(F32)
    is_o = (slot == ends[1:2]).astype(F32)
    plus, minus = is_c + is_o, is_c - is_o
    coords = stack3(jnp.concatenate([pool, jnp.zeros((4, 128), F32)], axis=0)[:, :64])
    at_c = unstack3(mm(coords, is_c.astype(BF16)), 8)
    at_o = unstack3(mm(coords, is_o.astype(BF16)), 8)
    diff = at_o - at_c
    dx, dy, dz = diff[0:1], diff[1:2], diff[2:3]
    squared = dx * dx + dy * dy + dz * dz
    scale = 1.0 / jnp.sqrt(1.0 + squared)
    ux, uy, uz = dx * scale, dy * scale, dz * scale
    length = jnp.sqrt(squared)
    step = length - 0.5 * iota((8, 256), 0).astype(F32)
    basis = jnp.exp(-2.0 * step * step)
    kinds = iota((8, 256), 0).astype(F32)
    hot_c = (at_c[3:4] == kinds).astype(F32)
    hot_o = (at_o[3:4] == kinds).astype(F32)
    harm = jnp.concatenate(
        [
            jnp.ones_like(ux), ROOT3 * ux * uy, ROOT3 * uy * uz, 0.5 * (3.0 * uz * uz - 1.0), ROOT3 * ux * uz,
            0.5 * ROOT3 * (ux * ux - uy * uy), ux, uy, uz, jnp.zeros((7, 256), F32),
        ],
        axis=0,
    )
    h1 = top(harm)
    h2 = top(harm - h1)
    b1 = top(basis)
    feat = jnp.concatenate(
        [
            b1, b1, basis - b1, hot_c, hot_c, hot_o, hot_o, jnp.zeros((8, 256), F32),
            h1, h2, harm - h1 - h2, jnp.zeros((16, 256), F32),
        ],
        axis=0,
    ).T.astype(BF16)
    hid[...] = silu(mm(feat, feat_w[...]))
    harm_x[...] = mm(feat, expand_w[...])

    put_p = jnp.concatenate([plus, plus], axis=1).astype(BF16)
    put_m = jnp.concatenate([minus, minus], axis=1).astype(BF16)

    def keep_hidden():
        hi, lo = split(hid[...])
        hid_cat[:, 0:512] = hi
        hid_cat[:, 512:1024] = lo
        hid_cat[:, 1024:1536] = hi

    keep_hidden()
    same = None
    copies = []
    for layer in range(2):
        w = mm(hid_cat[...], env_cat[layer])
        contrib = jnp.concatenate([w] * 5, axis=1) * harm_x[...]
        hi, lo = split(contrib)
        both = jnp.concatenate([hi, lo], axis=0)
        part_p, part_m = mm(put_p, both[:, :384]), mm(put_m, both[:, 384:])
        part = jnp.concatenate([part_p, part_m], axis=1)
        for k in range(8):
            send_part[layer, k] = part[32 + 4 * k : 36 + 4 * k]
        back = [
            remote(
                send_part.at[layer, k], got_part.at[layer, k], part_s.at[layer, k], part_r.at[layer, k], hosts[7 - k]
            )
            for k in range(8)
        ]
        for k in ORDER:
            back[k].start()
        copies += back
        if same is None:
            names_col = own.T[:, 4:5]
            same = (names_col[:64] == names).astype(F32)[:, :64]
            same = jnp.concatenate([same, same], axis=1).astype(BF16)
            get_p = jnp.concatenate([plus, plus], axis=0).T.astype(BF16)
            get_m = jnp.concatenate([minus, minus], axis=0).T.astype(BF16)
        pre[...] = mm(hid_cat[...], lat_cat[layer])
        for copy in back:
            copy.wait_recv()
        got = got_part[layer].reshape(32, 640)
        hi, lo = split(jnp.concatenate([part[:32], got], axis=0))
        env = mm(same, jnp.concatenate([hi, lo], axis=0))
        for k in range(8):
            send_env[layer, k] = env[32 + 4 * k : 36 + 4 * k]
        forth = [
            remote(send_env.at[layer, k], got_env.at[layer, k], env_s.at[layer, k], env_r.at[layer, k], hosts[k])
            for k in range(8)
        ]
        for k in ORDER:
            forth[k].start()
        copies += forth
        for copy in forth:
            copy.wait_recv()
        got = got_env[layer].reshape(32, 640)
        hi, lo = split(jnp.concatenate([env[:32], got], axis=0))
        both = jnp.concatenate([hi, lo], axis=0)
        prod = jnp.concatenate([mm(get_p, both[:, :384]), mm(get_m, both[:, 384:])], axis=1) * harm_x[...]
        t0, t1, t2, t3, t4 = [prod[:, 128 * i : 128 * i + 128] for i in range(5)]
        t12 = t1 + t2
        low = iota((256, 128), 1) < 64
        fold = jnp.where(low, t3 + pltpu.roll(t3, 64, 1) + t4, t12 + pltpu.roll(t12, 64, 1))
        hi, lo = split(jnp.concatenate([fold, t0], axis=1))
        hid[...] += silu(pre[...] + mm(jnp.concatenate([hi, lo, hi], axis=1), sca_cat[layer]))
        keep_hidden()

    hi, lo = split(silu(mm(hid_cat[...], out_cat[...])))
    loads[11].wait()
    h = head_v[...]
    hh = top(h)
    hw = jnp.concatenate([hh, h - hh, jnp.zeros((4, 512), F32)], axis=0).astype(BF16)
    by_hi, by_lo = mm_nt(hw, hi), mm_nt(hw, lo)
    heads = by_hi[0:2] + by_hi[2:4] + by_lo[0:2]
    push = heads[1:2]
    vals = jnp.concatenate([0.5 * heads[0:1], push * ux, push * uy, push * uz, jnp.zeros((4, 256), F32)], axis=0)
    vals = stack3(vals)
    tot_p, tot_m = unstack3(mm(vals, get_p), 8), unstack3(mm(vals, get_m), 8)
    tile_tot[...] = jnp.where(iota((4, 128), 0) == 0, tot_p[:4], tot_m[:4])
    last = [remote(tile_tot, got_tot.at[k], tot_s.at[k], tot_r.at[k], beside[7 - k]) for k in range(8)]
    last.append(remote(tile_tot, got_tot.at[8], tot_s.at[8], tot_r.at[8], beside[8]))
    for copy in last:
        copy.start()
    for copy in first + copies:
        copy.wait_send()
    keep_names.wait()
    for copy in last:
        copy.wait_recv()
    for copy in last:
        copy.wait_send()


def owner_kernel(tot_h, names_h, energy_h, force_h, tot_v, names_v, energy_v, force_v, sem):
    loads = [pltpu.make_async_copy(tot_h, tot_v, sem.at[0]), pltpu.make_async_copy(names_h, names_v, sem.at[1])]
    for load in loads:
        load.start()
    lane = iota((1, 128), 1)
    loads[1].wait()
    pick = (iota((32, 128), 0).astype(F32) == names_v[4:5]).astype(F32)
    loads[0].wait()
    total = jnp.where(lane < 32, tot_v[8], 0.0)
    for k in range(8):
        total = jnp.where((lane >= 32 + 4 * k) & (lane < 36 + 4 * k), tot_v[k], total)
    total = stack3(jnp.concatenate([total, jnp.zeros((4, 128), F32)], axis=0))
    out = unstack3(mm_nt(total, pick.astype(BF16)), 8)
    energy_v[...] = out[0:1]
    force_v[...] = out[1:4]
    stores = [pltpu.make_async_copy(energy_v, energy_h, sem.at[2]), pltpu.make_async_copy(force_v, force_h, sem.at[3])]
    for store in stores:
        store.start()
    for store in stores:
        store.wait()


def solution(mesh):
    nx, ny = mesh.shape["gx"], mesh.shape["gy"]

    def local(
        positions, species, atom_count, send_list, edges, centre_embed, neighbour_embed, radial_weight, env_weight,
        latent_weight, out_weight, head_weight,
    ):
        anywhere = pl.BlockSpec(memory_space=pl.ANY)
        dma = pltpu.SemaphoreType.DMA
        totals, names = pl.pallas_call(
            functools.partial(kernel, nx, ny),
            out_shape=(jax.ShapeDtypeStruct((9, 4, 128), F32), jax.ShapeDtypeStruct((8, 128), F32)),
            in_specs=[anywhere] * 12,
            out_specs=(anywhere, anywhere),
            scratch_shapes=[
                pltpu.VMEM((3, 32), F32), pltpu.VMEM((1, 32), jnp.int32), pltpu.SMEM((1,), jnp.int32),
                pltpu.VMEM((1, 4, 8), jnp.int32), pltpu.VMEM((1, 2, 256), jnp.int32),
                pltpu.VMEM((8, 512), F32), pltpu.VMEM((8, 512), F32), pltpu.VMEM((8, 512), F32),
                pltpu.VMEM((2, 64, 512), F32), pltpu.VMEM((2, 704, 512), F32), pltpu.VMEM((512, 512), F32),
                pltpu.VMEM((2, 512), F32), pltpu.VMEM((128, 512), BF16), pltpu.VMEM((128, 640), BF16), pltpu.VMEM((2, 1536, 128), BF16),
                pltpu.VMEM((2, 1536, 512), BF16), pltpu.VMEM((2, 768, 512), BF16), pltpu.VMEM((1536, 512), BF16),
                pltpu.VMEM((4, 128), F32), pltpu.VMEM((8, 128), F32), pltpu.VMEM((8, 4, 128), F32),
                pltpu.VMEM((8, 128), F32), pltpu.VMEM((1, 2, 256), jnp.int32),
                pltpu.VMEM((2, 8, 4, 640), F32), pltpu.VMEM((2, 8, 4, 640), F32),
                pltpu.VMEM((2, 8, 4, 640), F32), pltpu.VMEM((2, 8, 4, 640), F32),
                pltpu.VMEM((4, 128), F32),
                pltpu.VMEM((256, 1536), BF16), pltpu.VMEM((256, 512), F32), pltpu.VMEM((256, 512), F32),
                pltpu.VMEM((256, 640), F32),
                dma((12,)), dma((8,)), dma((8,)), dma((2,)), dma((2,)), dma((2, 8)), dma((2, 8)), dma((2, 8)),
                dma((2, 8)), dma((9,)), dma((9,)), dma((1,)),
            ],
            compiler_params=pltpu.CompilerParams(
                collective_id=0, has_side_effects=True, vmem_limit_bytes=64 * 1024 * 1024
            ),
            name="pair_network",
        )(
            positions, species.reshape(1, -1), atom_count, send_list.transpose(0, 2, 1), edges,
            centre_embed.T, neighbour_embed.T, radial_weight.T, env_weight, latent_weight.transpose(0, 2, 1),
            out_weight, head_weight,
        )
        energy, forces = pl.pallas_call(
            owner_kernel,
            out_shape=(jax.ShapeDtypeStruct((1, 32), F32), jax.ShapeDtypeStruct((3, 32), F32)),
            in_specs=[anywhere] * 2,
            out_specs=(anywhere, anywhere),
            scratch_shapes=[
                pltpu.VMEM((9, 4, 128), F32), pltpu.VMEM((8, 128), F32), pltpu.VMEM((1, 32), F32),
                pltpu.VMEM((3, 32), F32), dma((4,)),
            ],
            compiler_params=pltpu.CompilerParams(vmem_limit_bytes=64 * 1024 * 1024),
            name="owner_sums",
        )(totals, names)
        return energy.reshape(-1), forces

    placed = (
        P(None, ("gx", "gy")), P(("gx", "gy")), P(("gx", "gy")), P(("gx", "gy"), None, None),
        P(("gx", "gy"), None, None), P(), P(), P(), P(), P(), P(), P(),
    )
    return jax.shard_map(
        local, mesh=mesh, in_specs=placed, out_specs=(P(("gx", "gy")), P(None, ("gx", "gy"))), check_vma=False
    )
```

```python
import functools

import jax
import jax.numpy as jnp
from jax import lax
from jax.experimental import pallas as pl
from jax.experimental.pallas import tpu as pltpu
from jax.sharding import PartitionSpec as P

MESH = pl.DeviceIdType.MESH
F32 = jnp.float32
BF16 = jnp.bfloat16
OFFSETS = ((-1, -1), (-1, 0), (-1, 1), (0, -1), (0, 1), (1, -1), (1, 0), (1, 1))
AROUND = OFFSETS + ((0, 0),)
ORDER = (0, 2, 5, 7, 1, 6, 3, 4)
ROOT3 = 3.0 ** 0.5


def div(a, b):
    return lax.div(a, jnp.int32(b))


def rem(a, b):
    return lax.rem(a, jnp.int32(b))


def host(lx, ly):
    a, b = rem(lx + 46, 64), rem(ly + 2, 16)
    zi, yy, t = div(a, 8), rem(a, 8), div(b, 2)
    x = div(t, 2)
    z = rem(2 * zi + rem(t + x, 2) + 6, 16)
    y = rem(yy + rem(zi, 2) * (7 - 2 * yy) + 3, 8)
    return rem(z, 8) * 8 + y, x * 4 + div(z, 8) * 2 + rem(b, 2)


def column(gx, gy):
    y, x = rem(rem(gx, 8) + 5, 8), div(gy, 4)
    z = rem(rem(div(gy, 2), 2) * 8 + div(gx, 8) + 10, 16)
    zi = div(z, 2)
    a = 8 * zi + y + rem(zi, 2) * (7 - 2 * y)
    b = 4 * x + 2 * rem(z + x, 2) + rem(gy, 2)
    return rem(a + 18, 64), rem(b + 14, 16)


def iota(shape, dim):
    return lax.broadcasted_iota(jnp.int32, shape, dim)


def mm(a, b):
    return lax.dot_general(a, b, (((1,), (0,)), ((), ())), preferred_element_type=F32)


def mm_nt(a, b):
    return lax.dot_general(a, b, (((1,), (1,)), ((), ())), preferred_element_type=F32)


def top(x):
    return x.astype(BF16).astype(F32)


def split(x):
    hi = x.astype(BF16)
    return hi, (x - hi.astype(F32)).astype(BF16)


def stack3(x):
    a = top(x)
    b = top(x - a)
    return jnp.concatenate([a, b, x - a - b], axis=0).astype(BF16)


def unstack3(y, n):
    return y[:n] + y[n : 2 * n] + y[2 * n : 3 * n]


def silu(v):
    return v / (1.0 + jnp.exp(-v))


def picked_names(snd_v):
    lane = iota((1, 128), 1)
    spread_k = ((iota((8, 128), 1) - 32) // 4 == iota((8, 128), 0)) & (iota((8, 128), 1) >= 32)
    by_lane = mm(snd_v[0].astype(F32).astype(BF16), spread_k.astype(F32).astype(BF16))
    by_lane = jnp.where(iota((4, 128), 1) % 4 == iota((4, 128), 0), by_lane, 0.0)
    names = jnp.sum(by_lane, axis=0, keepdims=True)
    names = jnp.where(lane < 32, lane.astype(F32), jnp.where(lane < 64, names, -1.0))
    return names


def kernel(
    nx, ny, pos_h, spc_h, cnt_h, snd_h, edg_h, emb_c, emb_n, rad_w, env_w, lat_w, out_w, head_h,
    got_tot, names_h,
    pos_v, spc_v, cnt_v, snd_v, edg_v, embc_v, embn_v, rad_v, env_v, lat_v, out_v, head_v,
    feat_w, expand_w, env_cat, lat_cat, sca_cat, out_cat,
    tile_near, tile_own, got_near, got_own, got_edges,
    send_part, got_part, send_env, got_env, tile_tot,
    hid_cat, hid, pre, harm_x,
    w_sem, near_s, near_r, own_s, own_r, part_s, part_r, env_s, env_r, tot_s, tot_r, name_sem,
):
    gx, gy = lax.axis_index("gx"), lax.axis_index("gy")
    lx, ly = column(gx, gy)
    beside = [(rem(lx + dx + nx, nx), rem(ly + dy + ny, ny)) for dx, dy in AROUND]

    loads = [
        pltpu.make_async_copy(src, dst, w_sem.at[i])
        for i, (src, dst) in enumerate(
            (
                (pos_h, pos_v), (spc_h, spc_v), (cnt_h, cnt_v), (snd_h, snd_v), (edg_h, edg_v), (emb_c, embc_v),
                (emb_n, embn_v), (rad_w, rad_v), (env_w, env_v), (lat_w, lat_v), (out_w, out_v), (head_h, head_v),
            )
        )
    ]
    for load in loads[:5]:
        load.start()

    barrier = pltpu.get_barrier_semaphore()
    for k in (0, 2, 5, 7, 1, 6, 3, 4, 8):
        pl.semaphore_signal(barrier, inc=1, device_id=beside[k], device_id_type=MESH)
    for load in loads[5:]:
        load.start()

    targets = [host(rem(gx + dx + nx, nx), rem(gy + dy + ny, ny)) for dx, dy in AROUND]

    for load in loads[:5]:
        load.wait()
    lane = iota((1, 128), 1)
    names = picked_names(snd_v)
    pick = (iota((32, 128), 0).astype(F32) == names).astype(F32)
    atoms = jnp.concatenate([pos_v[...], spc_v[...].astype(F32), jnp.zeros((4, 32), F32)], axis=0)
    picked = unstack3(mm(stack3(atoms), pick.astype(BF16)), 8)
    tile_near[...] = picked[:4]
    count_row = jnp.full((1, 128), cnt_v[0], jnp.int32).astype(F32)
    tile_own[...] = jnp.concatenate([picked[:4], names, count_row, names, names], axis=0)
    keep_names = pltpu.make_async_copy(tile_own, names_h, name_sem.at[0])
    keep_names.start()

    pl.semaphore_wait(barrier, 9)

    def remote(src, dst, send_sem, recv_sem, device):
        return pltpu.make_async_remote_copy(
            src_ref=src, dst_ref=dst, send_sem=send_sem, recv_sem=recv_sem, device_id=device, device_id_type=MESH
        )

    first = [
        remote(edg_v, got_edges, own_s.at[0], own_r.at[0], targets[8]),
        remote(tile_own, got_own, own_s.at[1], own_r.at[1], targets[8]),
    ]
    first += [remote(tile_near, got_near.at[k], near_s.at[k], near_r.at[k], targets[k]) for k in range(8)]
    for i in (2, 4, 7, 9, 3, 8, 0, 1, 5, 6):
        first[i].start()

    hosts = [host(*b) for b in beside]

    for load in loads[5:8]:
        load.wait()
    r, c, n = rad_v[...], embc_v[...], embn_v[...]
    feat_w[...] = jnp.concatenate(
        [top(r), r - top(r), top(r), top(c), c - top(c), top(n), n - top(n), jnp.zeros((72, 512), F32)], axis=0
    ).astype(BF16)
    row, col = iota((128, 640), 0), iota((128, 640), 1)
    expand_w[...] = ((row >= 64) & (row < 112) & (row % 16 == col // 64)).astype(F32).astype(BF16)
    loads[8].wait()
    for layer in range(2):
        e = 0.25 * env_v[layer]
        hi, lo = split(jnp.concatenate([e, e], axis=0).T)
        env_cat[layer, 0:512] = hi
        env_cat[layer, 512:1024] = hi
        env_cat[layer, 1024:1536] = lo
    loads[9].wait()

    def cut_latent(i, carry):
        layer, at = i // 8, pl.multiple_of((i % 8) * 64, 64)
        hi, lo = split(lat_v[layer, pl.ds(at, 64), :])
        lat_cat[layer, pl.ds(at, 64), :] = hi
        lat_cat[layer, pl.ds(pl.multiple_of(512 + at, 64), 64), :] = hi
        lat_cat[layer, pl.ds(pl.multiple_of(1024 + at, 64), 64), :] = lo
        return carry

    lax.fori_loop(0, 16, cut_latent, 0)
    for layer in range(2):
        for i, at in enumerate((576, 640, 512, 640)):
            hi, lo = split(lat_v[layer, at : at + 64, :])
            sca_cat[layer, 64 * i : 64 * i + 64] = hi
            sca_cat[layer, 256 + 64 * i : 320 + 64 * i] = hi
            sca_cat[layer, 512 + 64 * i : 576 + 64 * i] = lo
    loads[10].wait()
    for i in range(4):
        hi, lo = split(out_v[128 * i : 128 * i + 128, :].T)
        out_cat[0:512, 128 * i : 128 * i + 128] = hi
        out_cat[512:1024, 128 * i : 128 * i + 128] = hi
        out_cat[1024:1536, 128 * i : 128 * i + 128] = lo

    for copy in first:
        copy.wait_recv()

    own = got_own[...]
    pool = jnp.where(lane < 32, own[:4], 0.0)
    for k in range(8):
        pool = jnp.where((lane >= 32 + 4 * k) & (lane < 36 + 4 * k), got_near[k], pool)
    names = own[4:5]
    live = iota((1, 256), 1).astype(F32) < 8.0 * jnp.concatenate([own[5:6], own[5:6]], axis=1)
    ends = got_edges[0]
    ends = jnp.where(ends < 32, ends, 92 - ends + 2 * (ends & 3))
    ends = jnp.where(live, ends, -1)
    slot = iota((64, 256), 0)
    is_c = (slot == ends[0:1]).astype(F32)
    is_o = (slot == ends[1:2]).astype(F32)
    plus, minus = is_c + is_o, is_c - is_o
    coords = stack3(jnp.concatenate([pool, jnp.zeros((4, 128), F32)], axis=0)[:, :64])
    at_c = unstack3(mm(coords, is_c.astype(BF16)), 8)
    at_o = unstack3(mm(coords, is_o.astype(BF16)), 8)
    diff = at_o - at_c
    dx, dy, dz = diff[0:1], diff[1:2], diff[2:3]
    squared = dx * dx + dy * dy + dz * dz
    scale = 1.0 / jnp.sqrt(1.0 + squared)
    ux, uy, uz = dx * scale, dy * scale, dz * scale
    length = jnp.sqrt(squared)
    step = length - 0.5 * iota((8, 256), 0).astype(F32)
    basis = jnp.exp(-2.0 * step * step)
    kinds = iota((8, 256), 0).astype(F32)
    hot_c = (at_c[3:4] == kinds).astype(F32)
    hot_o = (at_o[3:4] == kinds).astype(F32)
    harm = jnp.concatenate(
        [
            jnp.ones_like(ux), ROOT3 * ux * uy, ROOT3 * uy * uz, 0.5 * (3.0 * uz * uz - 1.0), ROOT3 * ux * uz,
            0.5 * ROOT3 * (ux * ux - uy * uy), ux, uy, uz, jnp.zeros((7, 256), F32),
        ],
        axis=0,
    )
    h1 = top(harm)
    h2 = top(harm - h1)
    b1 = top(basis)
    feat = jnp.concatenate(
        [
            b1, b1, basis - b1, hot_c, hot_c, hot_o, hot_o, jnp.zeros((8, 256), F32),
            h1, h2, harm - h1 - h2, jnp.zeros((16, 256), F32),
        ],
        axis=0,
    ).T.astype(BF16)
    hid[...] = silu(mm(feat, feat_w[...]))
    harm_x[...] = mm(feat, expand_w[...])

    put_p = jnp.concatenate([plus, plus], axis=1).astype(BF16)
    put_m = jnp.concatenate([minus, minus], axis=1).astype(BF16)

    def keep_hidden():
        hi, lo = split(hid[...])
        hid_cat[:, 0:512] = hi
        hid_cat[:, 512:1024] = lo
        hid_cat[:, 1024:1536] = hi

    keep_hidden()
    same = None
    copies = []
    for layer in range(2):
        w = mm(hid_cat[...], env_cat[layer])
        contrib = jnp.concatenate([w] * 5, axis=1) * harm_x[...]
        hi, lo = split(contrib)
        both = jnp.concatenate([hi, lo], axis=0)
        part_p, part_m = mm(put_p, both[:, :384]), mm(put_m, both[:, 384:])
        part = jnp.concatenate([part_p, part_m], axis=1)
        for k in range(8):
            send_part[layer, k] = part[32 + 4 * k : 36 + 4 * k]
        back = [
            remote(
                send_part.at[layer, k], got_part.at[layer, k], part_s.at[layer, k], part_r.at[layer, k], hosts[7 - k]
            )
            for k in range(8)
        ]
        for k in ORDER:
            back[k].start()
        copies += back
        if same is None:
            names_col = own.T[:, 4:5]
            same = (names_col[:64] == names).astype(F32)[:, :64]
            same = jnp.concatenate([same, same], axis=1).astype(BF16)
            get_p = jnp.concatenate([plus, plus], axis=0).T.astype(BF16)
            get_m = jnp.concatenate([minus, minus], axis=0).T.astype(BF16)
        pre[...] = mm(hid_cat[...], lat_cat[layer])
        for copy in back:
            copy.wait_recv()
        got = got_part[layer].reshape(32, 640)
        hi, lo = split(jnp.concatenate([part[:32], got], axis=0))
        env = mm(same, jnp.concatenate([hi, lo], axis=0))
        for k in range(8):
            send_env[layer, k] = env[32 + 4 * k : 36 + 4 * k]
        forth = [
            remote(send_env.at[layer, k], got_env.at[layer, k], env_s.at[layer, k], env_r.at[layer, k], hosts[k])
            for k in range(8)
        ]
        for k in ORDER:
            forth[k].start()
        copies += forth
        for copy in forth:
            copy.wait_recv()
        got = got_env[layer].reshape(32, 640)
        hi, lo = split(jnp.concatenate([env[:32], got], axis=0))
        both = jnp.concatenate([hi, lo], axis=0)
        prod = jnp.concatenate([mm(get_p, both[:, :384]), mm(get_m, both[:, 384:])], axis=1) * harm_x[...]
        t0, t1, t2, t3, t4 = [prod[:, 128 * i : 128 * i + 128] for i in range(5)]
        t12 = t1 + t2
        low = iota((256, 128), 1) < 64
        fold = jnp.where(low, t3 + pltpu.roll(t3, 64, 1) + t4, t12 + pltpu.roll(t12, 64, 1))
        hi, lo = split(jnp.concatenate([fold, t0], axis=1))
        hid[...] += silu(pre[...] + mm(jnp.concatenate([hi, lo, hi], axis=1), sca_cat[layer]))
        keep_hidden()

    hi, lo = split(silu(mm(hid_cat[...], out_cat[...])))
    loads[11].wait()
    h = head_v[...]
    hh = top(h)
    hw = jnp.concatenate([hh, h - hh, jnp.zeros((4, 512), F32)], axis=0).astype(BF16)
    by_hi, by_lo = mm_nt(hw, hi), mm_nt(hw, lo)
    heads = by_hi[0:2] + by_hi[2:4] + by_lo[0:2]
    push = heads[1:2]
    vals = jnp.concatenate([0.5 * heads[0:1], push * ux, push * uy, push * uz, jnp.zeros((4, 256), F32)], axis=0)
    vals = stack3(vals)
    tot_p, tot_m = unstack3(mm(vals, get_p), 8), unstack3(mm(vals, get_m), 8)
    tile_tot[...] = jnp.where(iota((4, 128), 0) == 0, tot_p[:4], tot_m[:4])
    last = [remote(tile_tot, got_tot.at[k], tot_s.at[k], tot_r.at[k], beside[7 - k]) for k in range(8)]
    last.append(remote(tile_tot, got_tot.at[8], tot_s.at[8], tot_r.at[8], beside[8]))
    for copy in last:
        copy.start()
    for copy in first + copies:
        copy.wait_send()
    keep_names.wait()
    for copy in last:
        copy.wait_recv()
    for copy in last:
        copy.wait_send()


def owner_kernel(tot_h, names_h, energy_h, force_h, tot_v, names_v, energy_v, force_v, sem):
    loads = [pltpu.make_async_copy(tot_h, tot_v, sem.at[0]), pltpu.make_async_copy(names_h, names_v, sem.at[1])]
    for load in loads:
        load.start()
    lane = iota((1, 128), 1)
    loads[1].wait()
    pick = (iota((32, 128), 0).astype(F32) == names_v[4:5]).astype(F32)
    loads[0].wait()
    total = jnp.where(lane < 32, tot_v[8], 0.0)
    for k in range(8):
        total = jnp.where((lane >= 32 + 4 * k) & (lane < 36 + 4 * k), tot_v[k], total)
    total = stack3(jnp.concatenate([total, jnp.zeros((4, 128), F32)], axis=0))
    out = unstack3(mm_nt(total, pick.astype(BF16)), 8)
    energy_v[...] = out[0:1]
    force_v[...] = out[1:4]
    stores = [pltpu.make_async_copy(energy_v, energy_h, sem.at[2]), pltpu.make_async_copy(force_v, force_h, sem.at[3])]
    for store in stores:
        store.start()
    for store in stores:
        store.wait()


def solution(mesh):
    nx, ny = mesh.shape["gx"], mesh.shape["gy"]

    def local(
        positions, species, atom_count, send_list, edges, centre_embed, neighbour_embed, radial_weight, env_weight,
        latent_weight, out_weight, head_weight,
    ):
        anywhere = pl.BlockSpec(memory_space=pl.ANY)
        dma = pltpu.SemaphoreType.DMA
        totals, names = pl.pallas_call(
            functools.partial(kernel, nx, ny),
            out_shape=(jax.ShapeDtypeStruct((9, 4, 128), F32), jax.ShapeDtypeStruct((8, 128), F32)),
            in_specs=[anywhere] * 12,
            out_specs=(anywhere, anywhere),
            scratch_shapes=[
                pltpu.VMEM((3, 32), F32), pltpu.VMEM((1, 32), jnp.int32), pltpu.SMEM((1,), jnp.int32),
                pltpu.VMEM((1, 4, 8), jnp.int32), pltpu.VMEM((1, 2, 256), jnp.int32),
                pltpu.VMEM((8, 512), F32), pltpu.VMEM((8, 512), F32), pltpu.VMEM((8, 512), F32),
                pltpu.VMEM((2, 64, 512), F32), pltpu.VMEM((2, 704, 512), F32), pltpu.VMEM((512, 512), F32),
                pltpu.VMEM((2, 512), F32), pltpu.VMEM((128, 512), BF16), pltpu.VMEM((128, 640), BF16), pltpu.VMEM((2, 1536, 128), BF16),
                pltpu.VMEM((2, 1536, 512), BF16), pltpu.VMEM((2, 768, 512), BF16), pltpu.VMEM((1536, 512), BF16),
                pltpu.VMEM((4, 128), F32), pltpu.VMEM((8, 128), F32), pltpu.VMEM((8, 4, 128), F32),
                pltpu.VMEM((8, 128), F32), pltpu.VMEM((1, 2, 256), jnp.int32),
                pltpu.VMEM((2, 8, 4, 640), F32), pltpu.VMEM((2, 8, 4, 640), F32),
                pltpu.VMEM((2, 8, 4, 640), F32), pltpu.VMEM((2, 8, 4, 640), F32),
                pltpu.VMEM((4, 128), F32),
                pltpu.VMEM((256, 1536), BF16), pltpu.VMEM((256, 512), F32), pltpu.VMEM((256, 512), F32),
                pltpu.VMEM((256, 640), F32),
                dma((12,)), dma((8,)), dma((8,)), dma((2,)), dma((2,)), dma((2, 8)), dma((2, 8)), dma((2, 8)),
                dma((2, 8)), dma((9,)), dma((9,)), dma((1,)),
            ],
            compiler_params=pltpu.CompilerParams(
                collective_id=0, has_side_effects=True, vmem_limit_bytes=64 * 1024 * 1024
            ),
            name="pair_network",
        )(
            positions, species.reshape(1, -1), atom_count, send_list.transpose(0, 2, 1), edges,
            centre_embed.T, neighbour_embed.T, radial_weight.T, env_weight, latent_weight.transpose(0, 2, 1),
            out_weight, head_weight,
        )
        energy, forces = pl.pallas_call(
            owner_kernel,
            out_shape=(jax.ShapeDtypeStruct((1, 32), F32), jax.ShapeDtypeStruct((3, 32), F32)),
            in_specs=[anywhere] * 2,
            out_specs=(anywhere, anywhere),
            scratch_shapes=[
                pltpu.VMEM((9, 4, 128), F32), pltpu.VMEM((8, 128), F32), pltpu.VMEM((1, 32), F32),
                pltpu.VMEM((3, 32), F32), dma((4,)),
            ],
            compiler_params=pltpu.CompilerParams(vmem_limit_bytes=64 * 1024 * 1024),
            name="owner_sums",
        )(totals, names)
        return energy.reshape(-1), forces

    placed = (
        P(None, ("gx", "gy")), P(("gx", "gy")), P(("gx", "gy")), P(("gx", "gy"), None, None),
        P(("gx", "gy"), None, None), P(), P(), P(), P(), P(), P(), P(),
    )
    return jax.shard_map(
        local, mesh=mesh, in_specs=placed, out_specs=(P(("gx", "gy")), P(None, ("gx", "gy"))), check_vma=False
    )
```

```python
import functools

import jax
import jax.numpy as jnp
from jax import lax
from jax.experimental import pallas as pl
from jax.experimental.pallas import tpu as pltpu
from jax.sharding import PartitionSpec as P

MESH = pl.DeviceIdType.MESH
F32 = jnp.float32
BF16 = jnp.bfloat16
OFFSETS = ((-1, -1), (-1, 0), (-1, 1), (0, -1), (0, 1), (1, -1), (1, 0), (1, 1))
AROUND = OFFSETS + ((0, 0),)
ORDER = (0, 2, 5, 7, 1, 6, 3, 4)
ROOT3 = 3.0 ** 0.5


def div(a, b):
    return lax.div(a, jnp.int32(b))


def rem(a, b):
    return lax.rem(a, jnp.int32(b))


def host(lx, ly):
    a, b = rem(lx + 46, 64), rem(ly + 2, 16)
    zi, yy, t = div(a, 8), rem(a, 8), div(b, 2)
    x = div(t, 2)
    z = rem(2 * zi + rem(t + x, 2) + 6, 16)
    y = rem(yy + rem(zi, 2) * (7 - 2 * yy) + 3, 8)
    return rem(z, 8) * 8 + y, x * 4 + div(z, 8) * 2 + rem(b, 2)


def column(gx, gy):
    y, x = rem(rem(gx, 8) + 5, 8), div(gy, 4)
    z = rem(rem(div(gy, 2), 2) * 8 + div(gx, 8) + 10, 16)
    zi = div(z, 2)
    a = 8 * zi + y + rem(zi, 2) * (7 - 2 * y)
    b = 4 * x + 2 * rem(z + x, 2) + rem(gy, 2)
    return rem(a + 18, 64), rem(b + 14, 16)


def iota(shape, dim):
    return lax.broadcasted_iota(jnp.int32, shape, dim)


def mm(a, b):
    return lax.dot_general(a, b, (((1,), (0,)), ((), ())), preferred_element_type=F32)


def mm_nt(a, b):
    return lax.dot_general(a, b, (((1,), (1,)), ((), ())), preferred_element_type=F32)


def top(x):
    return x.astype(BF16).astype(F32)


def split(x):
    hi = x.astype(BF16)
    return hi, (x - hi.astype(F32)).astype(BF16)


def stack3(x):
    a = top(x)
    b = top(x - a)
    return jnp.concatenate([a, b, x - a - b], axis=0).astype(BF16)


def unstack3(y, n):
    return y[:n] + y[n : 2 * n] + y[2 * n : 3 * n]


def silu(v):
    return v / (1.0 + jnp.exp(-v))


def picked_names(snd_v):
    lane = iota((1, 128), 1)
    spread_k = ((iota((8, 128), 1) - 32) // 4 == iota((8, 128), 0)) & (iota((8, 128), 1) >= 32)
    by_lane = mm(snd_v[0].astype(F32).astype(BF16), spread_k.astype(F32).astype(BF16))
    by_lane = jnp.where(iota((4, 128), 1) % 4 == iota((4, 128), 0), by_lane, 0.0)
    names = jnp.sum(by_lane, axis=0, keepdims=True)
    names = jnp.where(lane < 32, lane.astype(F32), jnp.where(lane < 64, names, -1.0))
    return names


def kernel(
    nx, ny, pos_h, spc_h, cnt_h, snd_h, edg_h, emb_c, emb_n, rad_w, env_w, lat_w, out_w, head_h,
    got_tot, names_h,
    pos_v, spc_v, cnt_v, snd_v, edg_v, embc_v, embn_v, rad_v, env_v, lat_v, out_v, head_v,
    feat_w, expand_w, env_cat, lat_cat, sca_cat, out_cat,
    tile_near, tile_own, got_near, got_own, got_edges,
    send_part, got_part, send_env, got_env, tile_tot,
    hid_cat, hid, pre, harm_x,
    w_sem, near_s, near_r, own_s, own_r, part_s, part_r, env_s, env_r, tot_s, tot_r, name_sem,
):
    gx, gy = lax.axis_index("gx"), lax.axis_index("gy")
    lx, ly = column(gx, gy)
    beside = [(rem(lx + dx + nx, nx), rem(ly + dy + ny, ny)) for dx, dy in AROUND]

    loads = [
        pltpu.make_async_copy(src, dst, w_sem.at[i])
        for i, (src, dst) in enumerate(
            (
                (pos_h, pos_v), (spc_h, spc_v), (cnt_h, cnt_v), (snd_h, snd_v), (edg_h, edg_v), (emb_c, embc_v),
                (emb_n, embn_v), (rad_w, rad_v), (env_w, env_v), (lat_w, lat_v), (out_w, out_v), (head_h, head_v),
            )
        )
    ]
    for load in loads[:5]:
        load.start()

    barrier = pltpu.get_barrier_semaphore()
    for k in (0, 2, 5, 7, 1, 6, 3, 4, 8):
        pl.semaphore_signal(barrier, inc=1, device_id=beside[k], device_id_type=MESH)
    for load in loads[5:]:
        load.start()

    targets = [host(rem(gx + dx + nx, nx), rem(gy + dy + ny, ny)) for dx, dy in AROUND]

    for load in loads[:5]:
        load.wait()
    lane = iota((1, 128), 1)
    names = picked_names(snd_v)
    pick = (iota((32, 128), 0).astype(F32) == names).astype(F32)
    atoms = jnp.concatenate([pos_v[...], spc_v[...].astype(F32), jnp.zeros((4, 32), F32)], axis=0)
    picked = unstack3(mm(stack3(atoms), pick.astype(BF16)), 8)
    tile_near[...] = picked[:4]
    count_row = jnp.full((1, 128), cnt_v[0], jnp.int32).astype(F32)
    tile_own[...] = jnp.concatenate([picked[:4], names, count_row, names, names], axis=0)
    keep_names = pltpu.make_async_copy(tile_own, names_h, name_sem.at[0])
    keep_names.start()

    pl.semaphore_wait(barrier, 9)

    def remote(src, dst, send_sem, recv_sem, device):
        return pltpu.make_async_remote_copy(
            src_ref=src, dst_ref=dst, send_sem=send_sem, recv_sem=recv_sem, device_id=device, device_id_type=MESH
        )

    first = [
        remote(edg_v, got_edges, own_s.at[0], own_r.at[0], targets[8]),
        remote(tile_own, got_own, own_s.at[1], own_r.at[1], targets[8]),
    ]
    first += [remote(tile_near, got_near.at[k], near_s.at[k], near_r.at[k], targets[k]) for k in range(8)]
    for i in (2, 4, 7, 9, 3, 8, 0, 1, 5, 6):
        first[i].start()

    hosts = [host(*b) for b in beside]

    for load in loads[5:8]:
        load.wait()
    r, c, n = rad_v[...], embc_v[...], embn_v[...]
    feat_w[...] = jnp.concatenate(
        [top(r), r - top(r), top(r), top(c), c - top(c), top(n), n - top(n), jnp.zeros((72, 512), F32)], axis=0
    ).astype(BF16)
    row, col = iota((128, 640), 0), iota((128, 640), 1)
    expand_w[...] = ((row >= 64) & (row < 112) & (row % 16 == col // 64)).astype(F32).astype(BF16)
    loads[8].wait()
    for layer in range(2):
        e = 0.25 * env_v[layer]
        hi, lo = split(jnp.concatenate([e, e], axis=0).T)
        env_cat[layer, 0:512] = hi
        env_cat[layer, 512:1024] = hi
        env_cat[layer, 1024:1536] = lo
    loads[9].wait()

    def cut_latent(i, carry):
        layer, at = i // 8, pl.multiple_of((i % 8) * 64, 64)
        hi, lo = split(lat_v[layer, pl.ds(at, 64), :])
        lat_cat[layer, pl.ds(at, 64), :] = hi
        lat_cat[layer, pl.ds(pl.multiple_of(512 + at, 64), 64), :] = hi
        lat_cat[layer, pl.ds(pl.multiple_of(1024 + at, 64), 64), :] = lo
        return carry

    lax.fori_loop(0, 16, cut_latent, 0)
    for layer in range(2):
        for i, at in enumerate((576, 640, 512, 640)):
            hi, lo = split(lat_v[layer, at : at + 64, :])
            sca_cat[layer, 64 * i : 64 * i + 64] = hi
            sca_cat[layer, 256 + 64 * i : 320 + 64 * i] = hi
            sca_cat[layer, 512 + 64 * i : 576 + 64 * i] = lo
    loads[10].wait()
    for i in range(4):
        hi, lo = split(out_v[128 * i : 128 * i + 128, :].T)
        out_cat[0:512, 128 * i : 128 * i + 128] = hi
        out_cat[512:1024, 128 * i : 128 * i + 128] = hi
        out_cat[1024:1536, 128 * i : 128 * i + 128] = lo

    for copy in first:
        copy.wait_recv()

    own = got_own[...]
    pool = jnp.where(lane < 32, own[:4], 0.0)
    for k in range(8):
        pool = jnp.where((lane >= 32 + 4 * k) & (lane < 36 + 4 * k), got_near[k], pool)
    names = own[4:5]
    live = iota((1, 256), 1).astype(F32) < 8.0 * jnp.concatenate([own[5:6], own[5:6]], axis=1)
    ends = got_edges[0]
    ends = jnp.where(ends < 32, ends, 92 - ends + 2 * (ends & 3))
    ends = jnp.where(live, ends, -1)
    slot = iota((64, 256), 0)
    is_c = (slot == ends[0:1]).astype(F32)
    is_o = (slot == ends[1:2]).astype(F32)
    plus, minus = is_c + is_o, is_c - is_o
    coords = stack3(jnp.concatenate([pool, jnp.zeros((4, 128), F32)], axis=0)[:, :64])
    at_c = unstack3(mm(coords, is_c.astype(BF16)), 8)
    at_o = unstack3(mm(coords, is_o.astype(BF16)), 8)
    diff = at_o - at_c
    dx, dy, dz = diff[0:1], diff[1:2], diff[2:3]
    squared = dx * dx + dy * dy + dz * dz
    scale = 1.0 / jnp.sqrt(1.0 + squared)
    ux, uy, uz = dx * scale, dy * scale, dz * scale
    length = jnp.sqrt(squared)
    step = length - 0.5 * iota((8, 256), 0).astype(F32)
    basis = jnp.exp(-2.0 * step * step)
    kinds = iota((8, 256), 0).astype(F32)
    hot_c = (at_c[3:4] == kinds).astype(F32)
    hot_o = (at_o[3:4] == kinds).astype(F32)
    harm = jnp.concatenate(
        [
            jnp.ones_like(ux), ROOT3 * ux * uy, ROOT3 * uy * uz, 0.5 * (3.0 * uz * uz - 1.0), ROOT3 * ux * uz,
            0.5 * ROOT3 * (ux * ux - uy * uy), ux, uy, uz, jnp.zeros((7, 256), F32),
        ],
        axis=0,
    )
    h1 = top(harm)
    h2 = top(harm - h1)
    b1 = top(basis)
    feat = jnp.concatenate(
        [
            b1, b1, basis - b1, hot_c, hot_c, hot_o, hot_o, jnp.zeros((8, 256), F32),
            h1, h2, harm - h1 - h2, jnp.zeros((16, 256), F32),
        ],
        axis=0,
    ).T.astype(BF16)
    hid[...] = silu(mm(feat, feat_w[...]))
    harm_x[...] = mm(feat, expand_w[...])

    put_p = jnp.concatenate([plus, plus], axis=1).astype(BF16)
    put_m = jnp.concatenate([minus, minus], axis=1).astype(BF16)

    def keep_hidden():
        hi, lo = split(hid[...])
        hid_cat[:, 0:512] = hi
        hid_cat[:, 512:1024] = lo
        hid_cat[:, 1024:1536] = hi

    keep_hidden()
    same = None
    copies = []
    for layer in range(2):
        w = mm(hid_cat[...], env_cat[layer])
        contrib = jnp.concatenate([w] * 5, axis=1) * harm_x[...]
        hi, lo = split(contrib)
        both = jnp.concatenate([hi, lo], axis=0)
        part_p, part_m = mm(put_p, both[:, :384]), mm(put_m, both[:, 384:])
        part = jnp.concatenate([part_p, part_m], axis=1)
        back = [
            remote(
                send_part.at[layer, k], got_part.at[layer, k], part_s.at[layer, k], part_r.at[layer, k], hosts[7 - k]
            )
            for k in range(8)
        ]
        for k in ORDER:
            send_part[layer, k] = part[32 + 4 * k : 36 + 4 * k]
            back[k].start()
        copies += back
        if same is None:
            names_col = own.T[:, 4:5]
            same = (names_col[:64] == names).astype(F32)[:, :64]
            same = jnp.concatenate([same, same], axis=1).astype(BF16)
            get_p = jnp.concatenate([plus, plus], axis=0).T.astype(BF16)
            get_m = jnp.concatenate([minus, minus], axis=0).T.astype(BF16)
        pre[...] = mm(hid_cat[...], lat_cat[layer])
        for copy in back:
            copy.wait_recv()
        got = got_part[layer].reshape(32, 640)
        hi, lo = split(jnp.concatenate([part[:32], got], axis=0))
        both = jnp.concatenate([hi, lo], axis=0)
        picks = mm(same[32:], both)
        forth = [
            remote(send_env.at[layer, k], got_env.at[layer, k], env_s.at[layer, k], env_r.at[layer, k], hosts[k])
            for k in range(8)
        ]
        for k in ORDER:
            send_env[layer, k] = picks[4 * k : 4 * k + 4]
            forth[k].start()
        env = mm(same[:32], both)
        copies += forth
        for copy in forth:
            copy.wait_recv()
        got = got_env[layer].reshape(32, 640)
        hi, lo = split(jnp.concatenate([env, got], axis=0))
        both = jnp.concatenate([hi, lo], axis=0)
        prod = jnp.concatenate([mm(get_p, both[:, :384]), mm(get_m, both[:, 384:])], axis=1) * harm_x[...]
        t0, t1, t2, t3, t4 = [prod[:, 128 * i : 128 * i + 128] for i in range(5)]
        t12 = t1 + t2
        low = iota((256, 128), 1) < 64
        fold = jnp.where(low, t3 + pltpu.roll(t3, 64, 1) + t4, t12 + pltpu.roll(t12, 64, 1))
        hi, lo = split(jnp.concatenate([fold, t0], axis=1))
        hid[...] += silu(pre[...] + mm(jnp.concatenate([hi, lo, hi], axis=1), sca_cat[layer]))
        keep_hidden()

    hi, lo = split(silu(mm(hid_cat[...], out_cat[...])))
    loads[11].wait()
    h = head_v[...]
    hh = top(h)
    hw = jnp.concatenate([hh, h - hh, jnp.zeros((4, 512), F32)], axis=0).astype(BF16)
    by_hi, by_lo = mm_nt(hw, hi), mm_nt(hw, lo)
    heads = by_hi[0:2] + by_hi[2:4] + by_lo[0:2]
    push = heads[1:2]
    vals = jnp.concatenate([0.5 * heads[0:1], push * ux, push * uy, push * uz, jnp.zeros((4, 256), F32)], axis=0)
    vals = stack3(vals)
    tot_p, tot_m = unstack3(mm(vals, get_p), 8), unstack3(mm(vals, get_m), 8)
    tile_tot[...] = jnp.where(iota((4, 128), 0) == 0, tot_p[:4], tot_m[:4])
    last = [remote(tile_tot, got_tot.at[k], tot_s.at[k], tot_r.at[k], beside[7 - k]) for k in range(8)]
    last.append(remote(tile_tot, got_tot.at[8], tot_s.at[8], tot_r.at[8], beside[8]))
    for copy in last:
        copy.start()
    for copy in first + copies:
        copy.wait_send()
    keep_names.wait()
    for copy in last:
        copy.wait_recv()
    for copy in last:
        copy.wait_send()


def owner_kernel(tot_h, names_h, energy_h, force_h, tot_v, names_v, energy_v, force_v, sem):
    loads = [pltpu.make_async_copy(tot_h, tot_v, sem.at[0]), pltpu.make_async_copy(names_h, names_v, sem.at[1])]
    for load in loads:
        load.start()
    lane = iota((1, 128), 1)
    loads[1].wait()
    pick = (iota((32, 128), 0).astype(F32) == names_v[4:5]).astype(F32)
    loads[0].wait()
    total = jnp.where(lane < 32, tot_v[8], 0.0)
    for k in range(8):
        total = jnp.where((lane >= 32 + 4 * k) & (lane < 36 + 4 * k), tot_v[k], total)
    total = stack3(jnp.concatenate([total, jnp.zeros((4, 128), F32)], axis=0))
    out = unstack3(mm_nt(total, pick.astype(BF16)), 8)
    energy_v[...] = out[0:1]
    force_v[...] = out[1:4]
    stores = [pltpu.make_async_copy(energy_v, energy_h, sem.at[2]), pltpu.make_async_copy(force_v, force_h, sem.at[3])]
    for store in stores:
        store.start()
    for store in stores:
        store.wait()


def solution(mesh):
    nx, ny = mesh.shape["gx"], mesh.shape["gy"]

    def local(
        positions, species, atom_count, send_list, edges, centre_embed, neighbour_embed, radial_weight, env_weight,
        latent_weight, out_weight, head_weight,
    ):
        anywhere = pl.BlockSpec(memory_space=pl.ANY)
        dma = pltpu.SemaphoreType.DMA
        totals, names = pl.pallas_call(
            functools.partial(kernel, nx, ny),
            out_shape=(jax.ShapeDtypeStruct((9, 4, 128), F32), jax.ShapeDtypeStruct((8, 128), F32)),
            in_specs=[anywhere] * 12,
            out_specs=(anywhere, anywhere),
            scratch_shapes=[
                pltpu.VMEM((3, 32), F32), pltpu.VMEM((1, 32), jnp.int32), pltpu.SMEM((1,), jnp.int32),
                pltpu.VMEM((1, 4, 8), jnp.int32), pltpu.VMEM((1, 2, 256), jnp.int32),
                pltpu.VMEM((8, 512), F32), pltpu.VMEM((8, 512), F32), pltpu.VMEM((8, 512), F32),
                pltpu.VMEM((2, 64, 512), F32), pltpu.VMEM((2, 704, 512), F32), pltpu.VMEM((512, 512), F32),
                pltpu.VMEM((2, 512), F32), pltpu.VMEM((128, 512), BF16), pltpu.VMEM((128, 640), BF16), pltpu.VMEM((2, 1536, 128), BF16),
                pltpu.VMEM((2, 1536, 512), BF16), pltpu.VMEM((2, 768, 512), BF16), pltpu.VMEM((1536, 512), BF16),
                pltpu.VMEM((4, 128), F32), pltpu.VMEM((8, 128), F32), pltpu.VMEM((8, 4, 128), F32),
                pltpu.VMEM((8, 128), F32), pltpu.VMEM((1, 2, 256), jnp.int32),
                pltpu.VMEM((2, 8, 4, 640), F32), pltpu.VMEM((2, 8, 4, 640), F32),
                pltpu.VMEM((2, 8, 4, 640), F32), pltpu.VMEM((2, 8, 4, 640), F32),
                pltpu.VMEM((4, 128), F32),
                pltpu.VMEM((256, 1536), BF16), pltpu.VMEM((256, 512), F32), pltpu.VMEM((256, 512), F32),
                pltpu.VMEM((256, 640), F32),
                dma((12,)), dma((8,)), dma((8,)), dma((2,)), dma((2,)), dma((2, 8)), dma((2, 8)), dma((2, 8)),
                dma((2, 8)), dma((9,)), dma((9,)), dma((1,)),
            ],
            compiler_params=pltpu.CompilerParams(
                collective_id=0, has_side_effects=True, vmem_limit_bytes=64 * 1024 * 1024
            ),
            name="pair_network",
        )(
            positions, species.reshape(1, -1), atom_count, send_list.transpose(0, 2, 1), edges,
            centre_embed.T, neighbour_embed.T, radial_weight.T, env_weight, latent_weight.transpose(0, 2, 1),
            out_weight, head_weight,
        )
        energy, forces = pl.pallas_call(
            owner_kernel,
            out_shape=(jax.ShapeDtypeStruct((1, 32), F32), jax.ShapeDtypeStruct((3, 32), F32)),
            in_specs=[anywhere] * 2,
            out_specs=(anywhere, anywhere),
            scratch_shapes=[
                pltpu.VMEM((9, 4, 128), F32), pltpu.VMEM((8, 128), F32), pltpu.VMEM((1, 32), F32),
                pltpu.VMEM((3, 32), F32), dma((4,)),
            ],
            compiler_params=pltpu.CompilerParams(vmem_limit_bytes=64 * 1024 * 1024),
            name="owner_sums",
        )(totals, names)
        return energy.reshape(-1), forces

    placed = (
        P(None, ("gx", "gy")), P(("gx", "gy")), P(("gx", "gy")), P(("gx", "gy"), None, None),
        P(("gx", "gy"), None, None), P(), P(), P(), P(), P(), P(), P(),
    )
    return jax.shard_map(
        local, mesh=mesh, in_specs=placed, out_specs=(P(("gx", "gy")), P(None, ("gx", "gy"))), check_vma=False
    )
```
